128 devices in a mesh: pb: 16 (over y, z), ta: 8 (over x, core).
Axes of the slice: x: 4, y: 4, z: 4, core: 2. Of those that a mesh axis runs over, the one named last changes fastest.
Arguments:
- coeffs: bfloat16 [128, 128, 16384], P('pb', None, 'ta'), may hold values from -6 to 6
- elph_table: bfloat16 [9, 16384], replicated, may hold values from -0.046875 to 0.046875
- energies: float32 [128, 128], replicated, may hold values from 1.6 to 1.7
- phonon_energy: float32 [9], replicated, may hold values from 0.005 to 0.035
- deviation: float32 [128, 128], replicated, may hold values from 0.2 to 2
- source: float32 [128, 128], P('pb'), may hold values from -6 to 6
- inv_tau: float32 [128, 128], P('pb'), may hold values from 0.5 to 5
- block_pairs: int32 [192, 2], replicated, may hold values from 0 to 127, as said below
- mode_index: int32 [192, 9], replicated, may hold values from 0 to 8, each once within a row
- offsets: int32 [192], replicated, may hold values from 0 to 16383
Outputs:
- new_deviation: float32 [128, 128], P('pb')
- linewidth: float32 [128, 128], P('pb')
The draws below stay inside these ranges and needn't reach their ends.
Inputs may be any that keep to these rules, and one draw needn't show every extreme that they name: `block_pairs`: block n lies on device n // 8 of pb. Exactly 12 pairs have their second block on each device; at most 24 pairs have their first block on one device, and one device has exactly 24. For one device of first blocks and one device of second blocks there are at most 2 pairs, and some such couple of devices has exactly 2 in every draw. `mode_index`: each row names every branch once.
All inputs are finite; a program needn't handle non-finite values.
Results may differ from the reference program's by a relative error of at most 0.0003.
Values may be sent and summed in bfloat16 or wider, within the bound.
A program may use at most 128 MiB of HBM per device.

```python
import math
import jax
import jax.numpy as jnp
from jax import lax

NMODE = 9
NT = 16384
BLK_DEV = 8
PAIRS_DEV = 12
ROWS = 128
NBLK = 128
PAIRS = 192


def draw_block_pairs(key, part):
    key = jax.random.fold_in(key, 11)
    keys = jax.random.split(key, 5)
    devices = NBLK // BLK_DEV
    total = PAIRS_DEV * devices
    busiest = 2 * PAIRS_DEV
    serial = jnp.arange(total, dtype=jnp.int32)
    row_perm = jax.random.permutation(keys[0], devices).astype(jnp.int32)
    col_perm = jax.random.permutation(keys[1], devices).astype(jnp.int32)
    row_slot = jnp.where(serial < busiest, 0, 1 + (serial - busiest) % (devices - 1))
    first_owner = row_perm[row_slot]
    second_owner = col_perm[serial % devices]
    first_block = first_owner * BLK_DEV + jax.random.randint(keys[2], (total,), 0, BLK_DEV, dtype=jnp.int32)
    second_block = second_owner * BLK_DEV + jax.random.randint(keys[3], (total,), 0, BLK_DEV, dtype=jnp.int32)
    shuffle = jax.random.permutation(keys[4], total)
    return jnp.stack([first_block, second_block], axis=1)[shuffle].astype(jnp.int32)


def plant(values, own_key, low, high):
    extent = values.shape
    index_at = [jax.random.randint(jax.random.fold_in(own_key, axis), (), 0, extent[axis]) for axis in range(len(extent))]
    values = values.at[tuple(index_at)].set(low)
    longest = extent.index(max(extent))
    index_at[longest] = (index_at[longest] + 1) % extent[longest]
    return values.at[tuple(index_at)].set(high)


def level_of(key, extent, cuts, smallest, high):
    level = 1.0
    for axis_at, shards_of in cuts:
        steps = jax.random.uniform(jax.random.fold_in(jax.random.fold_in(key, 6), axis_at), (shards_of,), jnp.float32, smallest / len(cuts), high / len(cuts))
        level = level * jnp.repeat(jnp.exp(steps), extent[axis_at] // shards_of).reshape((-1,) + (1,) * (len(extent) - 1 - axis_at))
    return level


def gaussian(stream_key, shape, width, reach, shards=(), kind=jnp.bfloat16):
    loudness = level_of(stream_key, shape, shards, -0.22, 0.18) if shards else 1.0
    values = jax.random.normal(stream_key, shape, jnp.float32) * width * loudness
    return jnp.minimum(jnp.maximum(values, -reach), reach).astype(kind)


def setup_inputs(seed: int = 0) -> dict:
    splits = jax.random.split(jax.random.key(seed), 11)
    coeffs = gaussian(splits[0], (NBLK, ROWS, NT), 1.0, 6.0, ((0, 16), (2, 8)))
    elph_table = gaussian(splits[1], (NMODE, NT), NT ** -0.5, 0.046875)
    energies = jnp.clip(jax.random.uniform(splits[2], (NBLK, ROWS), jnp.float32, 1.6, 1.7), 1.6, 1.7)
    phonon_energy = jnp.clip(jnp.exp(jax.random.uniform(splits[3], (NMODE,), jnp.float32, math.log(0.005), math.log(0.035))), 0.005, 0.035)
    deviation = jnp.clip(jax.random.uniform(splits[4], (NBLK, ROWS), jnp.float32, 0.2, 2.0), 0.2, 2.0)
    source = gaussian(splits[5], (NBLK, ROWS), 1.0, 6.0, ((0, 16),), jnp.float32)
    inv_tau = jnp.clip(jnp.exp(math.log(5.0) - 2.3025851 * jax.random.uniform(splits[6], (NBLK, ROWS), jnp.float32) ** level_of(splits[6], (NBLK, ROWS), ((0, 16),), -0.2, 0.2)), 0.5, 5.0)
    block_pairs = draw_block_pairs(jax.random.fold_in(splits[10], 71), 0)
    mode_index = jax.vmap(lambda own: jax.random.permutation(own, NMODE))(jax.random.split(splits[8], PAIRS)).reshape((PAIRS, NMODE)).astype(jnp.int32)
    offsets = plant(jax.random.randint(splits[9], (PAIRS,), 0, NT), jax.random.fold_in(splits[9], 1), 0, NT - 1).astype(jnp.int32)
    return {"coeffs": coeffs, "elph_table": elph_table, "energies": energies, "phonon_energy": phonon_energy, "deviation": deviation, "source": source, "inv_tau": inv_tau, "block_pairs": block_pairs, "mode_index": mode_index, "offsets": offsets}


BOLTZMANN_KT = 0.02585
BROADENING = 0.01


def pair_rates(coupling, energy_first, energy_second, phonon_energy):
    bose_factor = 1.0 / (jnp.exp(phonon_energy / BOLTZMANN_KT) - 1.0)
    detuning = energy_first[:, None] - energy_second[None, :]
    omega_mode = phonon_energy[:, None, None]
    lorentz_minus = 1.0 / (1.0 + ((detuning[None] - omega_mode) / BROADENING) ** 2)
    lorentz_plus = 1.0 / (1.0 + ((detuning[None] + omega_mode) / BROADENING) ** 2)
    strength = coupling * coupling / (coupling.shape[0] * coupling.shape[2])
    occupation = bose_factor[:, None, None]
    forward = strength * ((occupation + 1.0) * lorentz_minus + occupation * lorentz_plus)
    backward = strength * ((occupation + 1.0) * lorentz_plus + occupation * lorentz_minus)
    return forward, backward


def pair_flows(forward, backward, value_first, value_second):
    out_first = jnp.sum(forward, axis=(0, 2))
    in_first = jnp.sum(backward * value_second[None, None, :], axis=(0, 2))
    out_second = jnp.sum(backward, axis=(0, 1))
    in_second = jnp.sum(forward * value_first[None, :, None], axis=(0, 1))
    return out_first, in_first, out_second, in_second


def reference(coeffs, elph_table, energies, phonon_energy, deviation, source, inv_tau, block_pairs, mode_index, offsets):
    doubled = jnp.concatenate([elph_table, elph_table], axis=1)

    def one_pair(totals, pair_item):
        outflow, inflow = totals
        pair_blocks, mode_rows, offset_one = pair_item
        first_block = pair_blocks[0]
        second_block = pair_blocks[1]
        coeff_first = lax.dynamic_index_in_dim(coeffs, first_block, 0, keepdims=False)
        coeff_second = lax.dynamic_index_in_dim(coeffs, second_block, 0, keepdims=False)
        window = lax.dynamic_slice_in_dim(doubled, offset_one, NT, 1)
        coupling_table = jnp.take(window, mode_rows, axis=0)
        scaled = (coeff_first[None].astype(jnp.float32) * coupling_table[:, None, :].astype(jnp.float32)).astype(jnp.bfloat16)
        scaled_flat = scaled.reshape(NMODE * ROWS, NT)
        coupling = jnp.dot(scaled_flat, coeff_second.T, preferred_element_type=jnp.float32)
        coupling = coupling.reshape(NMODE, ROWS, ROWS)
        energy_first = lax.dynamic_index_in_dim(energies, first_block, 0, keepdims=False)
        energy_second = lax.dynamic_index_in_dim(energies, second_block, 0, keepdims=False)
        value_first = lax.dynamic_index_in_dim(deviation, first_block, 0, keepdims=False)
        value_second = lax.dynamic_index_in_dim(deviation, second_block, 0, keepdims=False)
        forward, backward = pair_rates(coupling, energy_first, energy_second, phonon_energy)
        out_first, in_first, out_second, in_second = pair_flows(forward, backward, value_first, value_second)
        outflow = outflow.at[first_block].add(out_first).at[second_block].add(out_second)
        inflow = inflow.at[first_block].add(in_first).at[second_block].add(in_second)
        return (outflow, inflow), None

    zeros_start = jnp.zeros((NBLK, ROWS), jnp.float32)
    (outflow, inflow), scan_rest = lax.scan(one_pair, (zeros_start, zeros_start), (block_pairs, mode_index, offsets))
    new_deviation = (source + inflow) / (inv_tau + outflow)
    return new_deviation, outflow
```

```python
import jax
import jax.numpy as jnp
from jax import lax
from jax.experimental import pallas as pl
from jax.experimental.pallas import tpu as pltpu
from jax.sharding import PartitionSpec as P

PAIRS_DEV = 12
BOLTZMANN_KT = 0.02585
BROADENING = 0.01
MESH = pl.DeviceIdType.MESH
LANES = 128
INTS = 5

MOVES = (
    (1, 0), (0, 1), (3, 0), (0, 3), (1, 1), (3, 3), (1, 3), (3, 1),
    (2, 0), (0, 2), (2, 1), (1, 2), (2, 3), (3, 2), (2, 2),
)


def pair_lists(block_pairs, mode_index, offsets, phonon_energy, block_count, low, trans_all):
    pair_total, mode_count = mode_index.shape
    start = lax.rem(offsets + low, trans_all)
    columns = (
        block_pairs[:, 0], block_pairs[:, 1], lax.rem(block_pairs[:, 1], block_count),
        lax.div(start, LANES), lax.rem(start, LANES),
    )
    owner = block_pairs[:, 1] // block_count
    serial = jnp.arange(pair_total, dtype=jnp.int32)
    earlier = (owner[:, None] == owner[None, :]) & (serial[None, :] < serial[:, None])
    slot = owner * PAIRS_DEV + jnp.sum(earlier.astype(jnp.int32), axis=1)
    hot = slot[None, :] == serial[:, None]
    data = jnp.concatenate([jnp.stack(columns, axis=1), mode_index], axis=1)
    data = jnp.sum(jnp.where(hot[:, :, None], data[None], 0), axis=1)
    modes = data[:, INTS:]
    rows = jnp.arange(mode_count, dtype=jnp.int32)
    at_row = modes[:, None, :] == rows[None, :, None]
    energy = jnp.sum(jnp.where(at_row, phonon_energy[None, None, :], 0.0), axis=2)
    bose = 1.0 / (jnp.exp(energy / BOLTZMANN_KT) - 1.0)
    values = jnp.concatenate([energy, bose], axis=1)
    return data[:, :INTS].reshape(-1), values.reshape(-1)


def kernel(
    ints, values, coeffs, table, energies, deviation, source, inv_tau,
    new_out, line_out,
    pieces, stage, other, part_out, part_in, weight_f, weight_b, value_a, wide, window,
    turn, acc_first, acc_second, first_in, second_in, total, total_in,
    send1, recv1, send2, recv2, send3, recv3, send4, recv4,
):
    blocks, rows, trans = coeffs.shape
    modes, trans_all = table.shape
    pair_count = other.shape[0]
    my_pb = lax.axis_index("pb")
    my_ta = lax.axis_index("ta")
    pb_count = 16
    ta_count = 8
    width = trans // pb_count
    strip = rows // ta_count
    my_y, my_z = my_pb // 4, my_pb % 4
    peers = [((my_y + dy) % 4) * 4 + (my_z + dz) % 4 for dy, dz in MOVES]
    mates = [(my_ta + d) % ta_count for d in range(1, ta_count)]
    n_peers, n_mates = len(peers), len(mates)

    barrier = pltpu.get_barrier_semaphore()
    for peer in peers:
        pl.semaphore_signal(barrier, inc=1, device_id=(peer, my_ta), device_id_type=MESH)
    for mate in mates:
        pl.semaphore_signal(barrier, inc=1, device_id=(my_pb, mate), device_id_type=MESH)
    pl.semaphore_wait(barrier, n_peers + n_mates)

    def remote(src, dst, send, recv, device):
        return pltpu.make_async_remote_copy(
            src_ref=src, dst_ref=dst, send_sem=send, recv_sem=recv,
            device_id=device, device_id_type=MESH,
        )

    my_lane = pl.multiple_of(my_pb * width, width)

    def spread(c, carry):
        for k, peer in enumerate(peers):
            lane = pl.multiple_of(peer * width, width)
            remote(
                coeffs.at[c, :, pl.ds(lane, width)], pieces.at[my_pb * blocks + c],
                send1.at[k], recv1.at[k], (peer, my_ta),
            ).start()
        pieces[my_pb * blocks + c] = coeffs[c, :, pl.ds(my_lane, width)]
        return carry

    lax.fori_loop(0, blocks, spread, 0)

    wide[...] = jnp.zeros_like(wide)
    tiles_all = trans_all // LANES

    def widen(tile, carry):
        lane = pl.multiple_of(lax.rem(tile, tiles_all) * LANES, LANES)
        wide[tile, pl.ds(0, modes), :] = table[:, pl.ds(lane, LANES)].astype(jnp.float32)
        return carry

    lax.fori_loop(0, wide.shape[0], widen, 0)
    acc_first[...] = jnp.zeros_like(acc_first)
    acc_second[...] = jnp.zeros_like(acc_second)

    def number(s, which):
        return ints[(my_pb * pair_count + s) * INTS + which]

    def strip_of(source_ref, block):
        row = source_ref[pl.ds(block, 1), :]
        turn[0] = jnp.transpose(jnp.broadcast_to(row, (rows, rows)))
        return turn[0, pl.ds(pl.multiple_of(my_ta * strip, strip), strip), :]

    def prepare(s, carry):
        first, second, tile, shift = number(s, 0), number(s, 1), number(s, 3), number(s, 4)
        tiles = trans // LANES
        piece = wide[pl.ds(tile, tiles + 1)]
        amount = jnp.full(piece.shape, shift, jnp.int32)
        for bit in range(7):
            moved = pltpu.roll(piece, LANES - (1 << bit), 2)
            piece = jnp.where((amount & (1 << bit)) != 0, moved, piece)
        lane = lax.broadcasted_iota(jnp.int32, (16, LANES), 1)
        keep = lane < LANES - amount[0]
        for t in range(tiles):
            window[s, :, t * LANES:(t + 1) * LANES] = jnp.where(keep, piece[t], piece[t + 1])
        detuning = strip_of(energies, first) - energies[pl.ds(second, 1), :]
        base = (my_pb * pair_count + s) * (2 * modes)
        for r in range(modes):
            energy = values[base + r]
            bose = values[base + modes + r]
            minus = 1.0 / (1.0 + ((detuning - energy) / BROADENING) ** 2)
            plus = 1.0 / (1.0 + ((detuning + energy) / BROADENING) ** 2)
            scale = 1.0 / (modes * rows)
            weight_f[s, r] = ((bose + 1.0) * minus + bose * plus) * scale
            weight_b[s, r] = ((bose + 1.0) * plus + bose * minus) * scale
        value_a[s] = strip_of(deviation, first)
        return carry

    lax.fori_loop(0, pair_count, prepare, 0)

    for k, peer in enumerate(peers):
        lane = pl.multiple_of(peer * width, width)
        copy = remote(
            coeffs.at[:, :, pl.ds(lane, width)], pieces.at[pl.ds(my_pb * blocks, blocks)],
            send1.at[k], recv1.at[k], (peer, my_ta),
        )
        copy.wait_send()
        copy.wait_recv()

    def deliver(s, carry):
        for k, peer in enumerate(peers):
            stage[s, k] = pieces[ints[(peer * pair_count + s) * INTS]]
            remote(
                stage.at[s, k], other.at[s, :, pl.ds(my_lane, width)],
                send2.at[s], recv2.at[s], (peer, my_ta),
            ).start()
        other[s, :, pl.ds(my_lane, width)] = pieces[number(s, 0)]
        return carry

    lax.fori_loop(0, pair_count, deliver, 0)

    def flows(s):
        copy = remote(
            part_in.at[s, pl.ds(0, n_mates)], part_in.at[s, pl.ds(0, n_mates)],
            send3.at[s], recv3.at[s], (my_pb, mates[0]),
        )
        copy.wait_send()
        copy.wait_recv()
        coupling = part_in[s, 0].astype(jnp.float32)
        for q in range(1, ta_count):
            coupling = coupling + part_in[s, q].astype(jnp.float32)
        square = coupling * coupling
        forward = jnp.sum(square * weight_f[s], axis=0)
        backward = jnp.sum(square * weight_b[s], axis=0)
        first, second = number(s, 0), number(s, 1)
        value_b = deviation[pl.ds(second, 1), :]
        out_first = jnp.sum(forward, axis=1, keepdims=True)
        in_first = jnp.sum(backward * value_b, axis=1, keepdims=True)
        out_second = jnp.sum(backward, axis=0, keepdims=True)
        in_second = jnp.sum(forward * value_a[s], axis=0, keepdims=True)
        here = lax.broadcasted_iota(jnp.int32, (strip, rows), 1) == first
        acc_first[0] += jnp.where(here, out_first, 0.0)
        acc_first[1] += jnp.where(here, in_first, 0.0)
        there = lax.broadcasted_iota(jnp.int32, (blocks, rows), 0) == number(s, 2)
        acc_second[0] += jnp.where(there, out_second, 0.0)
        acc_second[1] += jnp.where(there, in_second, 0.0)

    def couple(s, carry):
        copy = remote(
            stage.at[s], stage.at[s], send2.at[s], recv2.at[s], (peers[0], my_ta),
        )
        copy.wait_send()
        copy.wait_recv()
        place = number(s, 2)

        def one_mode(r, inner):
            row = window[s, pl.ds(r, 1), :]
            scale = jnp.broadcast_to(row, (16, trans)).astype(jnp.bfloat16)
            scaled = other[s].reshape(rows // 16, 16, trans) * scale[None]
            product = lax.dot_general(
                scaled.reshape(rows, trans), coeffs[place],
                (((1,), (1,)), ((), ())), preferred_element_type=jnp.float32,
            )
            part_out[s, r] = product.astype(jnp.bfloat16)
            return inner

        lax.fori_loop(0, modes, one_mode, 0)
        for mate in mates:
            remote(
                part_out.at[s, :, pl.ds(pl.multiple_of(mate * strip, strip), strip), :],
                part_in.at[s, my_ta], send3.at[s], recv3.at[s], (my_pb, mate),
            ).start()
        part_in[s, my_ta] = part_out[s, :, pl.ds(pl.multiple_of(my_ta * strip, strip), strip), :]

        @pl.when(s > 0)
        def _():
            flows(s - 1)

        return carry

    lax.fori_loop(0, pair_count, couple, 0)
    flows(pair_count - 1)

    for peer in peers:
        remote(acc_first, first_in.at[my_pb], send4.at[0], recv4.at[0], (peer, my_ta)).start()
    for mate in mates:
        remote(acc_second, second_in.at[my_ta], send4.at[1], recv4.at[1], (my_pb, mate)).start()
    first_in[my_pb] = acc_first[...]
    second_in[my_ta] = acc_second[...]
    copy = remote(
        first_in.at[pl.ds(0, n_peers)], first_in.at[pl.ds(0, n_peers)],
        send4.at[0], recv4.at[0], (peers[0], my_ta),
    )
    copy.wait_send()
    copy.wait_recv()
    total[...] = jnp.sum(first_in[...], axis=0)
    for mate in mates:
        remote(total, total_in.at[my_ta], send4.at[2], recv4.at[2], (my_pb, mate)).start()
    total_in[my_ta] = total[...]
    for ref, sem in ((second_in, 1), (total_in, 2)):
        copy = remote(
            ref.at[pl.ds(0, n_mates)], ref.at[pl.ds(0, n_mates)],
            send4.at[sem], recv4.at[sem], (my_pb, mates[0]),
        )
        copy.wait_send()
        copy.wait_recv()
    flow = []
    for c in range(2):
        turn[c] = jnp.transpose(total_in[:, c].reshape(rows, rows))
        mine = turn[c, pl.ds(pl.multiple_of(my_pb * blocks, blocks), blocks), :]
        flow.append(mine + jnp.sum(second_in[:, c], axis=0))
    line_out[...] = flow[0]
    new_out[...] = (source[...] + flow[1]) / (inv_tau[...] + flow[0])


def shards(
    coeffs,
    elph_table,
    energies,
    phonon_energy,
    deviation,
    source,
    inv_tau,
    block_pairs,
    mode_index,
    offsets,
):
    blocks, rows, trans = coeffs.shape
    modes, trans_all = elph_table.shape
    pb_count = lax.axis_size("pb")
    ta_count = lax.axis_size("ta")
    strip = rows // ta_count
    width = trans // pb_count
    low = lax.axis_index("ta") * trans
    ints, values = pair_lists(
        block_pairs, mode_index, offsets, phonon_energy, blocks, low, trans_all
    )
    smem = pl.BlockSpec(memory_space=pltpu.SMEM)
    vmem = pl.BlockSpec(memory_space=pltpu.VMEM)
    f32, bf16 = jnp.float32, jnp.bfloat16
    out = jax.ShapeDtypeStruct((blocks, rows), f32)
    dma = pltpu.SemaphoreType.DMA
    return pl.pallas_call(
        kernel,
        out_shape=(out, out),
        in_specs=[smem, smem] + [vmem] * 6,
        out_specs=(vmem, vmem),
        scratch_shapes=[
            pltpu.VMEM((pb_count * blocks, rows, width), bf16),
            pltpu.VMEM((PAIRS_DEV, pb_count - 1, rows, width), bf16),
            pltpu.VMEM((PAIRS_DEV, rows, trans), bf16),
            pltpu.VMEM((PAIRS_DEV, modes, rows, rows), bf16),
            pltpu.VMEM((PAIRS_DEV, ta_count, modes, strip, rows), bf16),
            pltpu.VMEM((PAIRS_DEV, modes, strip, rows), f32),
            pltpu.VMEM((PAIRS_DEV, modes, strip, rows), f32),
            pltpu.VMEM((PAIRS_DEV, strip, rows), f32),
            pltpu.VMEM(((trans_all + trans) // LANES + 1, 16, LANES), f32),
            pltpu.VMEM((PAIRS_DEV, 16, trans), f32),
            pltpu.VMEM((2, rows, rows), f32),
            pltpu.VMEM((2, strip, rows), f32),
            pltpu.VMEM((2, blocks, rows), f32),
            pltpu.VMEM((pb_count, 2, strip, rows), f32),
            pltpu.VMEM((ta_count, 2, blocks, rows), f32),
            pltpu.VMEM((2, strip, rows), f32),
            pltpu.VMEM((ta_count, 2, strip, rows), f32),
            dma((pb_count - 1,)), dma((pb_count - 1,)),
            dma((PAIRS_DEV,)), dma((PAIRS_DEV,)),
            dma((PAIRS_DEV,)), dma((PAIRS_DEV,)),
            dma((3,)), dma((3,)),
        ],
        compiler_params=pltpu.CompilerParams(
            collective_id=0, has_side_effects=True, vmem_limit_bytes=56 << 20
        ),
        name="rates",
    )(ints, values, coeffs, elph_table, energies, deviation, source, inv_tau)


def solution(mesh):
    in_specs = (
        P("pb", None, "ta"),
        P(),
        P(),
        P(),
        P(),
        P("pb", None),
        P("pb", None),
        P(),
        P(),
        P(),
    )
    out_specs = (P("pb", None), P("pb", None))
    return jax.shard_map(shards, mesh=mesh, in_specs=in_specs, out_specs=out_specs, check_vma=False)
```

```python
import jax
import jax.numpy as jnp
from jax import lax
from jax.experimental import pallas as pl
from jax.experimental.pallas import tpu as pltpu
from jax.sharding import PartitionSpec as P

PAIRS_DEV = 12
BOLTZMANN_KT = 0.02585
BROADENING = 0.01
MESH = pl.DeviceIdType.MESH
LANES = 128
TILE = 16
HALVES = 2
ROUND = 2
FIRST, SECOND, PLACE, START, SHIFT, MODE = range(6)

MOVES = (
    (1, 0), (0, 1), (3, 0), (0, 3), (1, 1), (3, 3), (1, 3), (3, 1),
    (2, 0), (0, 2), (2, 1), (1, 2), (2, 3), (3, 2), (2, 2),
)


def kernel(
    phonon, coeffs, table, energies, deviation, block_pairs, mode_index, offsets,
    flow_out,
    held, pieces_a, pieces_b, stage, other, scaled, part_out, part_in,
    weight_f, weight_b, value_a, wide, window, turn, lists, ints,
    acc_first, acc_second, first_out, first_in, second_in, total, total_in,
    local, send1, recv1, send2, recv2, send3, recv3, send4, recv4,
):
    blocks, rows, trans = coeffs.shape
    modes, trans_all = table.shape
    pair_total = block_pairs.shape[0]
    pair_count = other.shape[0]
    my_pb = lax.axis_index("pb")
    my_ta = lax.axis_index("ta")
    ta_count = part_in.shape[1]
    half = rows // HALVES
    strip = half // ta_count
    rounds = pair_count // ROUND
    my_y, my_z = my_pb // 4, my_pb % 4
    peers = [((my_y + dy) % 4) * 4 + (my_z + dz) % 4 for dy, dz in MOVES]
    mates = [(my_ta + d) % ta_count for d in range(1, ta_count)]
    n_peers, n_mates = len(peers), len(mates)
    pieces = (pieces_a, pieces_b)

    barrier = pltpu.get_barrier_semaphore()
    for peer in peers:
        pl.semaphore_signal(barrier, inc=1, device_id=(peer, my_ta), device_id_type=MESH)
    for mate in mates:
        pl.semaphore_signal(barrier, inc=1, device_id=(my_pb, mate), device_id_type=MESH)
    fetch = pltpu.make_async_copy(coeffs, held, local.at[0])
    fetch.start()
    pl.semaphore_wait(barrier, n_peers + n_mates)

    def remote(src, dst, send, recv, device):
        return pltpu.make_async_remote_copy(
            src_ref=src, dst_ref=dst, send_sem=send, recv_sem=recv,
            device_id=device, device_id_type=MESH,
        )

    my_lane = pl.multiple_of(my_pb * LANES, LANES)
    for h in range(HALVES):
        def spread(g, carry, h=h):
            for k, peer in enumerate(peers):
                lane = pl.multiple_of(peer * LANES, LANES)
                remote(
                    coeffs.at[pl.ds(ROUND * g, ROUND), pl.ds(h * half, half), pl.ds(lane, LANES)],
                    pieces[h].at[pl.ds(my_pb * blocks + ROUND * g, ROUND)],
                    send1.at[h, k], recv1.at[h, k], (peer, my_ta),
                ).start()
            return carry

        lax.fori_loop(0, blocks // ROUND, spread, 0)

    shift_of = blocks.bit_length() - 1
    second = block_pairs[:, 1:2]
    owner = lax.shift_right_logical(second, shift_of)
    serial = lax.broadcasted_iota(jnp.int32, (pair_total, LANES), 0)
    mine = (lax.broadcasted_iota(jnp.int32, (pair_total, LANES), 1) == owner).astype(jnp.int32)
    count = mine
    step = 1
    while step < pair_total:
        count = count + jnp.where(serial >= step, pltpu.roll(count, step, 0), 0)
        step *= 2
    rank = jnp.sum(mine * (count - 1), axis=1, keepdims=True)
    slot = owner * pair_count + rank
    spread_lanes = lists.shape[1]
    hot = lax.broadcasted_iota(jnp.int32, (pair_total, spread_lanes), 1) == slot
    lists[...] = jnp.zeros_like(lists)
    lists[0:1, 0:pair_total] = offsets[...]
    offset = jnp.transpose(jnp.broadcast_to(lists[0:1, :], (LANES, spread_lanes)))
    offset = offset[:pair_total, 0:1]
    start = offset + my_ta * trans
    start = jnp.where(start >= trans_all, start - trans_all, start)
    columns = [
        block_pairs[:, 0:1], second, second & (blocks - 1),
        lax.shift_right_logical(start, 7), start & (LANES - 1),
    ] + [mode_index[:, m:m + 1] for m in range(modes)]
    for c, column in enumerate(columns):
        lists[c:c + 1, :] = jnp.sum(jnp.where(hot, column, 0), axis=0, keepdims=True)
    listing = pltpu.make_async_copy(lists, ints, local.at[1])
    listing.start()
    fetch.wait()
    listing.wait()
    for h in range(HALVES):
        pieces[h][pl.ds(my_pb * blocks, blocks)] = held[:, pl.ds(h * half, half), pl.ds(my_lane, LANES)]

    def number(s, which):
        return ints[which, my_pb * pair_count + s]

    def hand_on(h):
        for k, peer in enumerate(peers):
            lane = pl.multiple_of(peer * LANES, LANES)
            copy = remote(
                coeffs.at[:, pl.ds(h * half, half), pl.ds(lane, LANES)],
                pieces[h].at[pl.ds(my_pb * blocks, blocks)],
                send1.at[h, k], recv1.at[h, k], (peer, my_ta),
            )
            copy.wait_send()
            copy.wait_recv()

        def deliver(g, carry):
            for k, peer in enumerate(peers):
                for u in range(ROUND):
                    stage[h, g, k, u] = pieces[h][ints[FIRST, peer * pair_count + ROUND * g + u]]
                remote(
                    stage.at[h, g, k],
                    other.at[pl.ds(ROUND * g, ROUND), pl.ds(h * half, half), pl.ds(my_lane, LANES)],
                    send2.at[h, g], recv2.at[h, g], (peer, my_ta),
                ).start()
            for u in range(ROUND):
                other[ROUND * g + u, pl.ds(h * half, half), pl.ds(my_lane, LANES)] = (
                    pieces[h][number(ROUND * g + u, FIRST)]
                )
            return carry

        lax.fori_loop(0, rounds, deliver, 0)

    hand_on(0)

    wide[...] = jnp.zeros_like(wide)
    tiles_all = trans_all // LANES
    tiles = trans // LANES

    def widen(tile, carry):
        lane = pl.multiple_of(lax.rem(tile, tiles_all) * LANES, LANES)
        wide[tile, pl.ds(0, modes), :] = table[:, pl.ds(lane, LANES)].astype(jnp.float32)
        return carry

    lax.fori_loop(0, wide.shape[0], widen, 0)
    acc_first[...] = jnp.zeros_like(acc_first)
    acc_second[...] = jnp.zeros_like(acc_second)

    def strips_of(source_ref, block):
        row = source_ref[pl.ds(block, 1), :]
        turn[...] = jnp.transpose(jnp.broadcast_to(row, (rows, rows)))
        return [
            turn[pl.ds(pl.multiple_of(h * half + my_ta * strip, strip), strip), :]
            for h in range(HALVES)
        ]

    def prepare(s, carry):
        first, second_one = number(s, FIRST), number(s, SECOND)
        piece = wide[pl.ds(number(s, START), tiles + 1)]
        amount = jnp.full(piece.shape, number(s, SHIFT), jnp.int32)
        for bit in range(7):
            moved = pltpu.roll(piece, LANES - (1 << bit), 2)
            piece = jnp.where((amount & (1 << bit)) != 0, moved, piece)
        keep = lax.broadcasted_iota(jnp.int32, (TILE, LANES), 1) < LANES - amount[0]
        for t in range(tiles):
            window[s, :, t * LANES:(t + 1) * LANES] = jnp.where(keep, piece[t], piece[t + 1])
        energy_b = energies[pl.ds(second_one, 1), :]
        energy_a = strips_of(energies, first)
        for h in range(HALVES):
            detuning = energy_a[h] - energy_b
            for m in range(modes):
                energy = jnp.full(detuning.shape, phonon[m], jnp.float32)
                bose = 1.0 / (jnp.exp(energy / BOLTZMANN_KT) - 1.0)
                minus = 1.0 / (1.0 + ((detuning - energy) / BROADENING) ** 2)
                plus = 1.0 / (1.0 + ((detuning + energy) / BROADENING) ** 2)
                scale = 1.0 / (modes * rows)
                weight_f[s, h, m] = ((bose + 1.0) * minus + bose * plus) * scale
                weight_b[s, h, m] = ((bose + 1.0) * plus + bose * minus) * scale
        for h, value in enumerate(strips_of(deviation, first)):
            value_a[s, h] = value
        return carry

    lax.fori_loop(0, pair_count, prepare, 0)
    for h in range(1, HALVES):
        hand_on(h)

    def flows(h, s):
        index = h * pair_count + s
        copy = remote(
            part_in.at[index, pl.ds(0, n_mates)], part_in.at[index, pl.ds(0, n_mates)],
            send3.at[index], recv3.at[index], (my_pb, mates[0]),
        )
        copy.wait_send()
        copy.wait_recv()
        coupling = part_in[index, 0].astype(jnp.float32)
        for q in range(1, ta_count):
            coupling = coupling + part_in[index, q].astype(jnp.float32)
        coupling = coupling[:modes * strip].reshape(modes, strip, rows)
        square = coupling * coupling
        forward = jnp.sum(square * weight_f[s, h], axis=0)
        backward = jnp.sum(square * weight_b[s, h], axis=0)
        value_b = deviation[pl.ds(number(s, SECOND), 1), :]
        out_first = jnp.sum(forward, axis=1, keepdims=True)
        in_first = jnp.sum(backward * value_b, axis=1, keepdims=True)
        out_second = jnp.sum(backward, axis=0, keepdims=True)
        in_second = jnp.sum(forward * value_a[s, h], axis=0, keepdims=True)
        here = lax.broadcasted_iota(jnp.int32, (strip, rows), 1) == number(s, FIRST)
        acc_first[0, h] += jnp.where(here, out_first, 0.0)
        acc_first[1, h] += jnp.where(here, in_first, 0.0)
        there = lax.broadcasted_iota(jnp.int32, (blocks, rows), 0) == number(s, PLACE)
        acc_second[0] += jnp.where(there, out_second, 0.0)
        acc_second[1] += jnp.where(there, in_second, 0.0)

    pad = part_out.shape[2] - modes * strip

    def couple(n, carry):
        h, g = n // rounds, n % rounds
        copy = remote(
            stage.at[h, g], stage.at[h, g], send2.at[h, g], recv2.at[h, g], (peers[0], my_ta),
        )
        copy.wait_send()
        copy.wait_recv()
        for u in range(ROUND):
            s = ROUND * g + u
            index = h * pair_count + s
            block = other[s, pl.ds(pl.multiple_of(h * half, half), half), :]
            block = block.reshape(half // TILE, TILE, trans)
            for m in range(modes):
                row = window[s, pl.ds(number(s, MODE + m), 1), :]
                scale = jnp.broadcast_to(row, (TILE, trans)).astype(jnp.bfloat16)
                scaled[m * half:(m + 1) * half, :] = (block * scale[None]).reshape(half, trans)
            product = lax.dot_general(
                scaled[...], held[number(s, PLACE)],
                (((1,), (1,)), ((), ())), preferred_element_type=jnp.float32,
            ).reshape(modes, ta_count, strip, rows)
            for q in range(ta_count):
                part = jnp.concatenate(
                    [product[:, q].reshape(modes * strip, rows), jnp.zeros((pad, rows), jnp.float32)], axis=0
                )
                part_out[index, q] = part.astype(jnp.bfloat16)
            for mate in mates:
                remote(
                    part_out.at[index, mate], part_in.at[index, my_ta],
                    send3.at[index], recv3.at[index], (my_pb, mate),
                ).start()
            part_in[index, my_ta] = part_out[index, my_ta]

        @pl.when(n > 0)
        def _():
            before_h, before_g = (n - 1) // rounds, (n - 1) % rounds
            for u in range(ROUND):
                flows(before_h, ROUND * before_g + u)

        return carry

    lax.fori_loop(0, HALVES * rounds, couple, 0)
    for u in range(ROUND):
        flows(HALVES - 1, pair_count - ROUND + u)

    used = 2 * HALVES * strip
    stacked = jnp.concatenate(
        [acc_first[...].reshape(used, rows), jnp.zeros((LANES - used, rows), jnp.float32)], axis=0
    )
    first_out[...] = jnp.transpose(stacked)
    for peer in peers:
        remote(
            first_out.at[pl.ds(pl.multiple_of(peer * blocks, blocks), blocks)], first_in.at[my_pb],
            send4.at[0], recv4.at[0], (peer, my_ta),
        ).start()
    for mate in mates:
        remote(acc_second, second_in.at[my_ta], send4.at[1], recv4.at[1], (my_pb, mate)).start()
    first_in[my_pb] = first_out[pl.ds(pl.multiple_of(my_pb * blocks, blocks), blocks)]
    second_in[my_ta] = acc_second[...]
    copy = remote(
        first_in.at[pl.ds(0, n_peers)], first_in.at[pl.ds(0, n_peers)],
        send4.at[0], recv4.at[0], (peers[0], my_ta),
    )
    copy.wait_send()
    copy.wait_recv()
    total[...] = jnp.sum(first_in[...], axis=0)
    for mate in mates:
        remote(total, total_in.at[my_ta], send4.at[2], recv4.at[2], (my_pb, mate)).start()
    total_in[my_ta] = total[...]
    for ref, sem in ((second_in, 1), (total_in, 2)):
        copy = remote(
            ref.at[pl.ds(0, n_mates)], ref.at[pl.ds(0, n_mates)],
            send4.at[sem], recv4.at[sem], (my_pb, mates[0]),
        )
        copy.wait_send()
        copy.wait_recv()
    lane = lax.broadcasted_iota(jnp.int32, (blocks, LANES), 1)
    for c in range(2):
        flow = jnp.sum(second_in[:, c], axis=0)
        for h in range(HALVES):
            low = (c * HALVES + h) * strip
            inside = (lane >= low) & (lane < low + strip)
            for q in range(ta_count):
                target = h * half + q * strip
                part = jnp.where(inside, total_in[q], 0.0)
                flow = flow + pltpu.roll(part, (target - low) % LANES, 1)
        flow_out[c] = flow


def shards(
    coeffs,
    elph_table,
    energies,
    phonon_energy,
    deviation,
    source,
    inv_tau,
    block_pairs,
    mode_index,
    offsets,
):
    blocks, rows, trans = coeffs.shape
    modes, trans_all = elph_table.shape
    pair_total = block_pairs.shape[0]
    pb_count = lax.axis_size("pb")
    ta_count = lax.axis_size("ta")
    half = rows // HALVES
    strip = half // ta_count
    rounds = PAIRS_DEV // ROUND
    units = HALVES * PAIRS_DEV
    padded = -(-modes * strip // TILE) * TILE
    list_lanes = -(-pair_total // LANES) * LANES
    smem = pl.BlockSpec(memory_space=pltpu.SMEM)
    vmem = pl.BlockSpec(memory_space=pltpu.VMEM)
    f32, bf16 = jnp.float32, jnp.bfloat16
    dma = pltpu.SemaphoreType.DMA
    flow = pl.pallas_call(
        kernel,
        out_shape=jax.ShapeDtypeStruct((2, blocks, rows), f32),
        in_specs=[smem, pl.BlockSpec(memory_space=pl.ANY)] + [vmem] * 6,
        out_specs=vmem,
        scratch_shapes=[
            pltpu.VMEM((blocks, rows, trans), bf16),
            pltpu.VMEM((pb_count * blocks, half, LANES), bf16),
            pltpu.VMEM((pb_count * blocks, half, LANES), bf16),
            pltpu.VMEM((HALVES, rounds, pb_count - 1, ROUND, half, LANES), bf16),
            pltpu.VMEM((PAIRS_DEV, rows, trans), bf16),
            pltpu.VMEM((modes * half, trans), bf16),
            pltpu.VMEM((units, ta_count, padded, rows), bf16),
            pltpu.VMEM((units, ta_count, padded, rows), bf16),
            pltpu.VMEM((PAIRS_DEV, HALVES, modes, strip, rows), f32),
            pltpu.VMEM((PAIRS_DEV, HALVES, modes, strip, rows), f32),
            pltpu.VMEM((PAIRS_DEV, HALVES, strip, rows), f32),
            pltpu.VMEM(((trans_all + trans) // LANES + 1, TILE, LANES), f32),
            pltpu.VMEM((PAIRS_DEV, TILE, trans), f32),
            pltpu.VMEM((rows, rows), f32),
            pltpu.VMEM((TILE, list_lanes), jnp.int32),
            pltpu.SMEM((TILE, list_lanes), jnp.int32),
            pltpu.VMEM((2, HALVES, strip, rows), f32),
            pltpu.VMEM((2, blocks, rows), f32),
            pltpu.VMEM((pb_count * blocks, LANES), f32),
            pltpu.VMEM((pb_count, blocks, LANES), f32),
            pltpu.VMEM((ta_count, 2, blocks, rows), f32),
            pltpu.VMEM((blocks, LANES), f32),
            pltpu.VMEM((ta_count, blocks, LANES), f32),
            dma((2,)),
            dma((HALVES, pb_count - 1)), dma((HALVES, pb_count - 1)),
            dma((HALVES, rounds)), dma((HALVES, rounds)),
            dma((units,)), dma((units,)),
            dma((3,)), dma((3,)),
        ],
        compiler_params=pltpu.CompilerParams(
            collective_id=0, has_side_effects=True, vmem_limit_bytes=56 << 20
        ),
        name="rates",
    )(
        phonon_energy, coeffs, elph_table, energies, deviation, block_pairs, mode_index,
        offsets.reshape(1, pair_total),
    )
    return (source + flow[1]) / (inv_tau + flow[0]), flow[0]


def solution(mesh):
    in_specs = (
        P("pb", None, "ta"),
        P(),
        P(),
        P(),
        P(),
        P("pb", None),
        P("pb", None),
        P(),
        P(),
        P(),
    )
    out_specs = (P("pb", None), P("pb", None))
    return jax.shard_map(shards, mesh=mesh, in_specs=in_specs, out_specs=out_specs, check_vma=False)
```

```python
import jax
import jax.numpy as jnp
from jax import lax
from jax.experimental import pallas as pl
from jax.experimental.pallas import tpu as pltpu
from jax.sharding import PartitionSpec as P

PAIRS_DEV = 12
BOLTZMANN_KT = 0.02585
BROADENING = 0.01
MESH = pl.DeviceIdType.MESH
LANES = 128
TILE = 16
HALVES = 2
ROUND = 2
FIRST, SECOND, PLACE, START, SHIFT, MODE = range(6)

MOVES = (
    (1, 0), (0, 1), (2, 2), (3, 0), (0, 3), (2, 1), (1, 1), (1, 2),
    (3, 3), (2, 3), (1, 3), (3, 2), (3, 1), (2, 0), (0, 2),
)
FAR_MOVES = (
    (2, 2), (2, 1), (1, 2), (2, 3), (3, 2), (1, 1), (3, 3), (1, 3),
    (3, 1), (2, 0), (0, 2), (1, 0), (0, 1), (3, 0), (0, 3),
)
MATES = (4, 3, 5, 2, 6, 1, 7)


def kernel(
    phonon, coeffs, table, energies, deviation, block_pairs, mode_index, offsets,
    flow_out,
    held, pieces_a, pieces_b, stage, other, scaled, part_out, part_in,
    weight_f, weight_b, value_a, wide, window, turn, lists, ints,
    acc_first, acc_second, first_out, first_in, second_in, total, total_in,
    local, send1, recv1, send2, recv2, send3, recv3, send4, recv4,
):
    blocks, rows, trans = coeffs.shape
    modes, trans_all = table.shape
    pair_total = block_pairs.shape[1]
    rounds = other.shape[1]
    pair_count = rounds * ROUND
    my_pb = lax.axis_index("pb")
    my_ta = lax.axis_index("ta")
    ta_count = part_in.shape[1]
    half = rows // HALVES
    strip = half // ta_count
    my_y, my_z = my_pb // 4, my_pb % 4
    peers = [((my_y + dy) % 4) * 4 + (my_z + dz) % 4 for dy, dz in MOVES]
    far_peers = [((my_y + dy) % 4) * 4 + (my_z + dz) % 4 for dy, dz in FAR_MOVES]
    mates = [(my_ta + d) % ta_count for d in MATES]
    n_peers, n_mates = len(peers), len(mates)
    pieces = (pieces_a, pieces_b)

    barrier = pltpu.get_barrier_semaphore()
    for peer in peers:
        pl.semaphore_signal(barrier, inc=1, device_id=(peer, my_ta), device_id_type=MESH)
    for mate in mates:
        pl.semaphore_signal(barrier, inc=1, device_id=(my_pb, mate), device_id_type=MESH)
    fetch = pltpu.make_async_copy(coeffs, held, local.at[0])
    fetch.start()
    pl.semaphore_wait(barrier, n_peers + n_mates)

    def remote(src, dst, send, recv, device):
        return pltpu.make_async_remote_copy(
            src_ref=src, dst_ref=dst, send_sem=send, recv_sem=recv,
            device_id=device, device_id_type=MESH,
        )

    my_lane = pl.multiple_of(my_pb * LANES, LANES)
    for h in range(HALVES):
        def spread(g, carry, h=h):
            for k, peer in enumerate(peers):
                lane = pl.multiple_of(peer * LANES, LANES)
                remote(
                    coeffs.at[pl.ds(ROUND * g, ROUND), pl.ds(h * half, half), pl.ds(lane, LANES)],
                    pieces[h].at[pl.ds(my_pb * blocks + ROUND * g, ROUND)],
                    send1.at[h, k], recv1.at[h, k], (peer, my_ta),
                ).start()
            return carry

        lax.fori_loop(0, blocks // ROUND, spread, 0)

    shift_of = blocks.bit_length() - 1
    spread_lanes = lists.shape[1]
    lists[...] = jnp.zeros_like(lists)
    lists[0:2, 0:pair_total] = block_pairs[...]
    lists[2:3, 0:pair_total] = offsets[...]
    lists[MODE:MODE + modes, 0:pair_total] = mode_index[...]
    column_form = jnp.transpose(lists[...])[:pair_total]
    second = column_form[:, 1:2]
    owner = lax.shift_right_logical(second, shift_of)
    serial = lax.broadcasted_iota(jnp.int32, (pair_total, LANES), 0)
    mine = (lax.broadcasted_iota(jnp.int32, (pair_total, LANES), 1) == owner).astype(jnp.int32)
    count = mine
    step = 1
    while step < pair_total:
        count = count + jnp.where(serial >= step, pltpu.roll(count, step, 0), 0)
        step *= 2
    rank = jnp.sum(mine * (count - 1), axis=1, keepdims=True)
    slot = owner * pair_count + rank
    hot = lax.broadcasted_iota(jnp.int32, (pair_total, spread_lanes), 1) == slot
    start = column_form[:, 2:3] + my_ta * trans
    start = jnp.where(start >= trans_all, start - trans_all, start)
    columns = [
        column_form[:, 0:1], second, second & (blocks - 1),
        lax.shift_right_logical(start, 7), start & (LANES - 1),
    ] + [column_form[:, MODE + m:MODE + m + 1] for m in range(modes)]
    for c, column in enumerate(columns):
        lists[c:c + 1, :] = jnp.sum(jnp.where(hot, column, 0), axis=0, keepdims=True)
    listing = pltpu.make_async_copy(lists.at[pl.ds(0, TILE)], ints, local.at[1])
    listing.start()
    fetch.wait()
    listing.wait()
    for h in range(HALVES):
        pieces[h][pl.ds(my_pb * blocks, blocks)] = held[:, pl.ds(h * half, half), pl.ds(my_lane, LANES)]

    def number(s, which):
        return ints[which, my_pb * pair_count + s]

    def hand_on(h):
        for k, peer in enumerate(peers):
            lane = pl.multiple_of(peer * LANES, LANES)
            copy = remote(
                coeffs.at[:, pl.ds(h * half, half), pl.ds(lane, LANES)],
                pieces[h].at[pl.ds(my_pb * blocks, blocks)],
                send1.at[h, k], recv1.at[h, k], (peer, my_ta),
            )
            copy.wait_recv()

        def deliver(g, carry):
            for k, peer in enumerate(peers):
                for u in range(ROUND):
                    stage[h, g, k, u] = pieces[h][ints[FIRST, peer * pair_count + ROUND * g + u]]
                remote(
                    stage.at[h, g, k],
                    other.at[h, g, my_pb],
                    send2.at[h, g], recv2.at[h, g], (peer, my_ta),
                ).start()
            for u in range(ROUND):
                other[h, g, my_pb, u] = pieces[h][number(ROUND * g + u, FIRST)]
            return carry

        lax.fori_loop(0, rounds, deliver, 0)

    hand_on(0)

    wide[...] = jnp.zeros_like(wide)
    tiles_all = trans_all // LANES
    tiles = trans // LANES

    def widen(tile, carry):
        lane = pl.multiple_of(lax.rem(tile, tiles_all) * LANES, LANES)
        wide[tile, pl.ds(0, modes), :] = table[:, pl.ds(lane, LANES)].astype(jnp.float32)
        return carry

    lax.fori_loop(0, wide.shape[0], widen, 0)
    acc_first[...] = jnp.zeros_like(acc_first)
    acc_second[...] = jnp.zeros_like(acc_second)

    def strips_of(source_ref, block):
        row = source_ref[pl.ds(block, 1), :]
        turn[...] = jnp.transpose(jnp.broadcast_to(row, (rows, rows)))
        return [
            turn[pl.ds(pl.multiple_of(h * half + my_ta * strip, strip), strip), :]
            for h in range(HALVES)
        ]

    def prepare(s, carry):
        first, second_one = number(s, FIRST), number(s, SECOND)
        piece = wide[pl.ds(number(s, START), tiles + 1)]
        amount = jnp.full(piece.shape, number(s, SHIFT), jnp.int32)
        for bit in range(7):
            moved = pltpu.roll(piece, LANES - (1 << bit), 2)
            piece = jnp.where((amount & (1 << bit)) != 0, moved, piece)
        keep = lax.broadcasted_iota(jnp.int32, (TILE, LANES), 1) < LANES - amount[0]
        for t in range(tiles):
            window[s, :, t * LANES:(t + 1) * LANES] = jnp.where(keep, piece[t], piece[t + 1])
        energy_b = energies[pl.ds(second_one, 1), :]
        energy_a = strips_of(energies, first)
        for h in range(HALVES):
            detuning = energy_a[h] - energy_b
            for m in range(modes):
                energy = jnp.full(detuning.shape, phonon[m], jnp.float32)
                bose = 1.0 / (jnp.exp(energy / BOLTZMANN_KT) - 1.0)
                minus = 1.0 / (1.0 + ((detuning - energy) / BROADENING) ** 2)
                plus = 1.0 / (1.0 + ((detuning + energy) / BROADENING) ** 2)
                scale = 1.0 / (modes * rows)
                weight_f[s, h, m] = ((bose + 1.0) * minus + bose * plus) * scale
                weight_b[s, h, m] = ((bose + 1.0) * plus + bose * minus) * scale
        for h, value in enumerate(strips_of(deviation, first)):
            value_a[s, h] = value
        return carry

    lax.fori_loop(0, pair_count, prepare, 0)
    for h in range(1, HALVES):
        hand_on(h)

    def flows(h, s):
        index = h * pair_count + s
        copy = remote(
            part_in.at[index, pl.ds(0, n_mates)], part_in.at[index, pl.ds(0, n_mates)],
            send3.at[index], recv3.at[index], (my_pb, mates[0]),
        )
        copy.wait_recv()
        coupling = part_in[index, 0].astype(jnp.float32)
        for q in range(1, ta_count):
            coupling = coupling + part_in[index, q].astype(jnp.float32)
        coupling = coupling[:modes * strip].reshape(modes, strip, rows)
        square = coupling * coupling
        forward = jnp.sum(square * weight_f[s, h], axis=0)
        backward = jnp.sum(square * weight_b[s, h], axis=0)
        value_b = deviation[pl.ds(number(s, SECOND), 1), :]
        out_first = jnp.sum(forward, axis=1, keepdims=True)
        in_first = jnp.sum(backward * value_b, axis=1, keepdims=True)
        out_second = jnp.sum(backward, axis=0, keepdims=True)
        in_second = jnp.sum(forward * value_a[s, h], axis=0, keepdims=True)
        here = lax.broadcasted_iota(jnp.int32, (strip, rows), 1) == number(s, FIRST)
        acc_first[0, h] += jnp.where(here, out_first, 0.0)
        acc_first[1, h] += jnp.where(here, in_first, 0.0)
        there = lax.broadcasted_iota(jnp.int32, (blocks, rows), 0) == number(s, PLACE)
        acc_second[0] += jnp.where(there, out_second, 0.0)
        acc_second[1] += jnp.where(there, in_second, 0.0)

    pad = part_out.shape[2] - modes * strip

    def flows_of(n):
        for u in range(ROUND):
            flows(n // rounds, ROUND * (n % rounds) + u)

    def couple(n, carry):
        h, g = n // rounds, n % rounds

        @pl.when(n > 1)
        def _():
            flows_of(n - 2)

        copy = remote(
            stage.at[h, g], stage.at[h, g], send2.at[h, g], recv2.at[h, g], (peers[0], my_ta),
        )
        copy.wait_recv()
        for u in range(ROUND):
            s = ROUND * g + u
            index = h * pair_count + s
            for m in range(modes):
                row = window[s, pl.ds(number(s, MODE + m), 1), :]
                scale = jnp.broadcast_to(row, (TILE, trans)).astype(jnp.bfloat16)
                for t in range(tiles):
                    block = other[h, g, t, u].reshape(half // TILE, TILE, LANES)
                    block = block * scale[None, :, t * LANES:(t + 1) * LANES]
                    scaled[m * half:(m + 1) * half, t * LANES:(t + 1) * LANES] = block.reshape(half, LANES)
            product = lax.dot_general(
                scaled[...], held[number(s, PLACE)],
                (((1,), (1,)), ((), ())), preferred_element_type=jnp.float32,
            ).reshape(modes, ta_count, strip, rows)
            for q in range(ta_count):
                part = jnp.concatenate(
                    [product[:, q].reshape(modes * strip, rows), jnp.zeros((pad, rows), jnp.float32)], axis=0
                )
                part_out[index, q] = part.astype(jnp.bfloat16)
            for mate in mates:
                remote(
                    part_out.at[index, mate], part_in.at[index, my_ta],
                    send3.at[index], recv3.at[index], (my_pb, mate),
                ).start()
            part_in[index, my_ta] = part_out[index, my_ta]
        return carry

    lax.fori_loop(0, HALVES * rounds, couple, 0)
    for n in range(HALVES * rounds - 2, HALVES * rounds):
        flows_of(n)

    used = 2 * HALVES * strip
    stacked = jnp.concatenate(
        [acc_first[...].reshape(used, rows), jnp.zeros((LANES - used, rows), jnp.float32)], axis=0
    )
    first_out[...] = jnp.transpose(stacked)
    for peer in far_peers:
        remote(
            first_out.at[pl.ds(pl.multiple_of(peer * blocks, blocks), blocks)], first_in.at[my_pb],
            send4.at[0], recv4.at[0], (peer, my_ta),
        ).start()
    for mate in mates:
        remote(acc_second, second_in.at[my_ta], send4.at[1], recv4.at[1], (my_pb, mate)).start()
    first_in[my_pb] = first_out[pl.ds(pl.multiple_of(my_pb * blocks, blocks), blocks)]
    second_in[my_ta] = acc_second[...]

    for h in range(HALVES):
        for k, peer in enumerate(peers):
            lane = pl.multiple_of(peer * LANES, LANES)
            remote(
                coeffs.at[:, pl.ds(h * half, half), pl.ds(lane, LANES)],
                pieces[h].at[pl.ds(my_pb * blocks, blocks)],
                send1.at[h, k], recv1.at[h, k], (peer, my_ta),
            ).wait_send()

    def sent(n, carry):
        h, g = n // rounds, n % rounds
        remote(
            stage.at[h, g], stage.at[h, g], send2.at[h, g], recv2.at[h, g], (peers[0], my_ta),
        ).wait_send()
        for u in range(ROUND):
            index = ROUND * n + u
            block = part_in.at[index, pl.ds(0, n_mates)]
            remote(block, block, send3.at[index], recv3.at[index], (my_pb, mates[0])).wait_send()
        return carry

    lax.fori_loop(0, HALVES * rounds, sent, 0)

    few = first_in.at[pl.ds(0, n_peers)]
    sums = remote(few, few, send4.at[0], recv4.at[0], (peers[0], my_ta))
    sums.wait_recv()
    total[...] = jnp.sum(first_in[...], axis=0)
    for mate in mates:
        remote(total, total_in.at[my_ta], send4.at[2], recv4.at[2], (my_pb, mate)).start()
    total_in[my_ta] = total[...]
    sums.wait_send()
    for ref, sem in ((second_in, 1), (total_in, 2)):
        few = ref.at[pl.ds(0, n_mates)]
        copy = remote(few, few, send4.at[sem], recv4.at[sem], (my_pb, mates[0]))
        copy.wait_send()
        copy.wait_recv()
    lane = lax.broadcasted_iota(jnp.int32, (blocks, LANES), 1)
    for c in range(2):
        flow = jnp.sum(second_in[:, c], axis=0)
        for h in range(HALVES):
            low = (c * HALVES + h) * strip
            inside = (lane >= low) & (lane < low + strip)
            for q in range(ta_count):
                target = h * half + q * strip
                part = jnp.where(inside, total_in[q], 0.0)
                flow = flow + pltpu.roll(part, (target - low) % LANES, 1)
        flow_out[c] = flow


def shards(
    coeffs,
    elph_table,
    energies,
    phonon_energy,
    deviation,
    source,
    inv_tau,
    block_pairs,
    mode_index,
    offsets,
):
    blocks, rows, trans = coeffs.shape
    modes, trans_all = elph_table.shape
    pair_total = block_pairs.shape[0]
    pb_count = lax.axis_size("pb")
    ta_count = lax.axis_size("ta")
    half = rows // HALVES
    strip = half // ta_count
    rounds = PAIRS_DEV // ROUND
    units = HALVES * PAIRS_DEV
    padded = -(-modes * strip // TILE) * TILE
    list_lanes = -(-pair_total // LANES) * LANES
    smem = pl.BlockSpec(memory_space=pltpu.SMEM)
    vmem = pl.BlockSpec(memory_space=pltpu.VMEM)
    f32, bf16 = jnp.float32, jnp.bfloat16
    dma = pltpu.SemaphoreType.DMA
    flow = pl.pallas_call(
        kernel,
        out_shape=jax.ShapeDtypeStruct((2, blocks, rows), f32),
        in_specs=[smem, pl.BlockSpec(memory_space=pl.ANY)] + [vmem] * 6,
        out_specs=vmem,
        scratch_shapes=[
            pltpu.VMEM((blocks, rows, trans), bf16),
            pltpu.VMEM((pb_count * blocks, half, LANES), bf16),
            pltpu.VMEM((pb_count * blocks, half, LANES), bf16),
            pltpu.VMEM((HALVES, rounds, pb_count - 1, ROUND, half, LANES), bf16),
            pltpu.VMEM((HALVES, rounds, pb_count, ROUND, half, LANES), bf16),
            pltpu.VMEM((modes * half, trans), bf16),
            pltpu.VMEM((units, ta_count, padded, rows), bf16),
            pltpu.VMEM((units, ta_count, padded, rows), bf16),
            pltpu.VMEM((PAIRS_DEV, HALVES, modes, strip, rows), f32),
            pltpu.VMEM((PAIRS_DEV, HALVES, modes, strip, rows), f32),
            pltpu.VMEM((PAIRS_DEV, HALVES, strip, rows), f32),
            pltpu.VMEM(((trans_all + trans) // LANES + 1, TILE, LANES), f32),
            pltpu.VMEM((PAIRS_DEV, TILE, trans), f32),
            pltpu.VMEM((rows, rows), f32),
            pltpu.VMEM((LANES, list_lanes), jnp.int32),
            pltpu.SMEM((TILE, list_lanes), jnp.int32),
            pltpu.VMEM((2, HALVES, strip, rows), f32),
            pltpu.VMEM((2, blocks, rows), f32),
            pltpu.VMEM((pb_count * blocks, LANES), f32),
            pltpu.VMEM((pb_count, blocks, LANES), f32),
            pltpu.VMEM((ta_count, 2, blocks, rows), f32),
            pltpu.VMEM((blocks, LANES), f32),
            pltpu.VMEM((ta_count, blocks, LANES), f32),
            dma((2,)),
            dma((HALVES, pb_count - 1)), dma((HALVES, pb_count - 1)),
            dma((HALVES, rounds)), dma((HALVES, rounds)),
            dma((units,)), dma((units,)),
            dma((3,)), dma((3,)),
        ],
        compiler_params=pltpu.CompilerParams(
            collective_id=0, has_side_effects=True, vmem_limit_bytes=56 << 20
        ),
        name="rates",
    )(
        phonon_energy, coeffs, elph_table, energies, deviation, block_pairs.T, mode_index.T,
        offsets.reshape(1, pair_total),
    )
    return (source + flow[1]) / (inv_tau + flow[0]), flow[0]


def solution(mesh):
    in_specs = (
        P("pb", None, "ta"),
        P(),
        P(),
        P(),
        P(),
        P("pb", None),
        P("pb", None),
        P(),
        P(),
        P(),
    )
    out_specs = (P("pb", None), P("pb", None))
    return jax.shard_map(shards, mesh=mesh, in_specs=in_specs, out_specs=out_specs, check_vma=False)
```

```python
import jax
import jax.numpy as jnp
from jax import lax
from jax.experimental import pallas as pl
from jax.experimental.pallas import tpu as pltpu
from jax.sharding import PartitionSpec as P

PAIRS_DEV = 12
BOLTZMANN_KT = 0.02585
BROADENING = 0.01
MESH = pl.DeviceIdType.MESH
LANES = 128
TILE = 16
HALVES = 2
ROUND = 2
SINGLE = 4
LAG = 3
FIRST, SECOND, PLACE, START, SHIFT, MODE = range(6)

MOVES = (
    (1, 0), (0, 1), (2, 2), (3, 0), (0, 3), (2, 1), (1, 1), (1, 2),
    (3, 3), (2, 3), (1, 3), (3, 2), (3, 1), (2, 0), (0, 2),
)
FAR_MOVES = (
    (2, 2), (2, 1), (1, 2), (2, 3), (3, 2), (1, 1), (3, 3), (1, 3),
    (3, 1), (2, 0), (0, 2), (1, 0), (0, 1), (3, 0), (0, 3),
)
MATES = (4, 3, 5, 2, 6, 1, 7)


def kernel(
    phonon, coeffs, table, energies, deviation, block_pairs, mode_index, offsets,
    flow_out,
    held, pieces_a, pieces_b, stage, other, scaled, part_out, part_in,
    weight_f, weight_b, value_a, wide, window, turn, lists, ints,
    acc_first, acc_second, first_out, first_in, second_in, total, total_in,
    local, send1, recv1, send2, recv2, send3, recv3, send4, recv4,
):
    blocks, rows, trans = coeffs.shape
    modes, trans_all = table.shape
    pair_total = block_pairs.shape[1]
    pair_count = other.shape[1]
    paired = HALVES * pair_count - SINGLE
    my_pb = lax.axis_index("pb")
    my_ta = lax.axis_index("ta")
    ta_count = part_in.shape[1]
    half = rows // HALVES
    strip = half // ta_count
    my_y, my_z = my_pb // 4, my_pb % 4
    peers = [((my_y + dy) % 4) * 4 + (my_z + dz) % 4 for dy, dz in MOVES]
    far_peers = [((my_y + dy) % 4) * 4 + (my_z + dz) % 4 for dy, dz in FAR_MOVES]
    mates = [(my_ta + d) % ta_count for d in MATES]
    n_peers, n_mates = len(peers), len(mates)
    pieces = (pieces_a, pieces_b)

    barrier = pltpu.get_barrier_semaphore()
    for peer in peers:
        pl.semaphore_signal(barrier, inc=1, device_id=(peer, my_ta), device_id_type=MESH)
    for mate in mates:
        pl.semaphore_signal(barrier, inc=1, device_id=(my_pb, mate), device_id_type=MESH)
    fetch = pltpu.make_async_copy(coeffs, held, local.at[0])
    fetch.start()
    pl.semaphore_wait(barrier, n_peers + n_mates)

    def remote(src, dst, send, recv, device):
        return pltpu.make_async_remote_copy(
            src_ref=src, dst_ref=dst, send_sem=send, recv_sem=recv,
            device_id=device, device_id_type=MESH,
        )

    my_lane = pl.multiple_of(my_pb * LANES, LANES)
    for h in range(HALVES):
        def spread(g, carry, h=h):
            for k, peer in enumerate(peers):
                lane = pl.multiple_of(peer * LANES, LANES)
                remote(
                    coeffs.at[pl.ds(ROUND * g, ROUND), pl.ds(h * half, half), pl.ds(lane, LANES)],
                    pieces[h].at[pl.ds(my_pb * blocks + ROUND * g, ROUND)],
                    send1.at[h, k], recv1.at[h, k], (peer, my_ta),
                ).start()
            return carry

        lax.fori_loop(0, blocks // ROUND, spread, 0)

    shift_of = blocks.bit_length() - 1
    spread_lanes = lists.shape[1]
    lists[...] = jnp.zeros_like(lists)
    lists[0:2, 0:pair_total] = block_pairs[...]
    lists[2:3, 0:pair_total] = offsets[...]
    lists[MODE:MODE + modes, 0:pair_total] = mode_index[...]
    column_form = jnp.transpose(lists[...])[:pair_total]
    second = column_form[:, 1:2]
    owner = lax.shift_right_logical(second, shift_of)
    serial = lax.broadcasted_iota(jnp.int32, (pair_total, LANES), 0)
    mine = (lax.broadcasted_iota(jnp.int32, (pair_total, LANES), 1) == owner).astype(jnp.int32)
    count = mine
    step = 1
    while step < pair_total:
        count = count + jnp.where(serial >= step, pltpu.roll(count, step, 0), 0)
        step *= 2
    rank = jnp.sum(mine * (count - 1), axis=1, keepdims=True)
    slot = owner * pair_count + rank
    hot = lax.broadcasted_iota(jnp.int32, (pair_total, spread_lanes), 1) == slot
    start = column_form[:, 2:3] + my_ta * trans
    start = jnp.where(start >= trans_all, start - trans_all, start)
    columns = [
        column_form[:, 0:1], second, second & (blocks - 1),
        lax.shift_right_logical(start, 7), start & (LANES - 1),
    ] + [column_form[:, MODE + m:MODE + m + 1] for m in range(modes)]
    for c, column in enumerate(columns):
        lists[c:c + 1, :] = jnp.sum(jnp.where(hot, column, 0), axis=0, keepdims=True)
    listing = pltpu.make_async_copy(lists.at[pl.ds(0, TILE)], ints, local.at[1])
    listing.start()
    fetch.wait()
    listing.wait()
    for h in range(HALVES):
        pieces[h][pl.ds(my_pb * blocks, blocks)] = held[:, pl.ds(h * half, half), pl.ds(my_lane, LANES)]

    def number(s, which):
        return ints[which, my_pb * pair_count + s]

    def hand_on(h):
        for k, peer in enumerate(peers):
            lane = pl.multiple_of(peer * LANES, LANES)
            copy = remote(
                coeffs.at[:, pl.ds(h * half, half), pl.ds(lane, LANES)],
                pieces[h].at[pl.ds(my_pb * blocks, blocks)],
                send1.at[h, k], recv1.at[h, k], (peer, my_ta),
            )
            copy.wait_recv()

        def deliver(s, count):
            for k, peer in enumerate(peers):
                for u in range(count):
                    stage[h, s + u, k] = pieces[h][ints[FIRST, peer * pair_count + s + u]]
                remote(
                    stage.at[h, pl.ds(s, count), k], other.at[h, pl.ds(s, count), my_pb],
                    send2.at[h, s], recv2.at[h, s], (peer, my_ta),
                ).start()
            for u in range(count):
                other[h, s + u, my_pb] = pieces[h][number(s + u, FIRST)]

        def deliver_round(g, carry):
            deliver(ROUND * g, ROUND)
            return carry

        def deliver_one(s, carry):
            deliver(s, 1)
            return carry

        singles = SINGLE if h == HALVES - 1 else 0
        lax.fori_loop(0, (pair_count - singles) // ROUND, deliver_round, 0)
        lax.fori_loop(pair_count - singles, pair_count, deliver_one, 0)

    hand_on(0)

    wide[...] = jnp.zeros_like(wide)
    tiles_all = trans_all // LANES
    tiles = trans // LANES

    def widen(tile, carry):
        lane = pl.multiple_of(lax.rem(tile, tiles_all) * LANES, LANES)
        wide[tile, pl.ds(0, modes), :] = table[:, pl.ds(lane, LANES)].astype(jnp.float32)
        return carry

    lax.fori_loop(0, wide.shape[0], widen, 0)
    acc_first[...] = jnp.zeros_like(acc_first)
    acc_second[...] = jnp.zeros_like(acc_second)

    def strips_of(source_ref, block):
        row = source_ref[pl.ds(block, 1), :]
        turn[...] = jnp.transpose(jnp.broadcast_to(row, (rows, rows)))
        return [
            turn[pl.ds(pl.multiple_of(h * half + my_ta * strip, strip), strip), :]
            for h in range(HALVES)
        ]

    def prepare(s, carry):
        first, second_one = number(s, FIRST), number(s, SECOND)
        piece = wide[pl.ds(number(s, START), tiles + 1)]
        amount = jnp.full(piece.shape, number(s, SHIFT), jnp.int32)
        for bit in range(7):
            moved = pltpu.roll(piece, LANES - (1 << bit), 2)
            piece = jnp.where((amount & (1 << bit)) != 0, moved, piece)
        keep = lax.broadcasted_iota(jnp.int32, (TILE, LANES), 1) < LANES - amount[0]
        for t in range(tiles):
            window[s, :, t * LANES:(t + 1) * LANES] = jnp.where(keep, piece[t], piece[t + 1])
        energy_b = energies[pl.ds(second_one, 1), :]
        energy_a = strips_of(energies, first)
        for h in range(HALVES):
            detuning = energy_a[h] - energy_b
            for m in range(modes):
                energy = jnp.full(detuning.shape, phonon[m], jnp.float32)
                bose = 1.0 / (jnp.exp(energy / BOLTZMANN_KT) - 1.0)
                minus = 1.0 / (1.0 + ((detuning - energy) / BROADENING) ** 2)
                plus = 1.0 / (1.0 + ((detuning + energy) / BROADENING) ** 2)
                scale = 1.0 / (modes * rows)
                weight_f[s, h, m] = ((bose + 1.0) * minus + bose * plus) * scale
                weight_b[s, h, m] = ((bose + 1.0) * plus + bose * minus) * scale
        for h, value in enumerate(strips_of(deviation, first)):
            value_a[s, h] = value
        return carry

    lax.fori_loop(0, pair_count, prepare, 0)
    for h in range(1, HALVES):
        hand_on(h)

    def flows(h, s):
        index = h * pair_count + s
        copy = remote(
            part_in.at[index, pl.ds(0, n_mates)], part_in.at[index, pl.ds(0, n_mates)],
            send3.at[index], recv3.at[index], (my_pb, mates[0]),
        )
        copy.wait_recv()
        coupling = part_in[index, 0].astype(jnp.float32)
        for q in range(1, ta_count):
            coupling = coupling + part_in[index, q].astype(jnp.float32)
        coupling = coupling[:modes * strip].reshape(modes, strip, rows)
        square = coupling * coupling
        forward = jnp.sum(square * weight_f[s, h], axis=0)
        backward = jnp.sum(square * weight_b[s, h], axis=0)
        value_b = deviation[pl.ds(number(s, SECOND), 1), :]
        out_first = jnp.sum(forward, axis=1, keepdims=True)
        in_first = jnp.sum(backward * value_b, axis=1, keepdims=True)
        out_second = jnp.sum(backward, axis=0, keepdims=True)
        in_second = jnp.sum(forward * value_a[s, h], axis=0, keepdims=True)
        here = lax.broadcasted_iota(jnp.int32, (strip, rows), 1) == number(s, FIRST)
        acc_first[0, h] += jnp.where(here, out_first, 0.0)
        acc_first[1, h] += jnp.where(here, in_first, 0.0)
        there = lax.broadcasted_iota(jnp.int32, (blocks, rows), 0) == number(s, PLACE)
        acc_second[0] += jnp.where(there, out_second, 0.0)
        acc_second[1] += jnp.where(there, in_second, 0.0)

    pad = part_out.shape[2] - modes * strip

    def arrival(n, act):
        h, s = n // pair_count, n % pair_count

        def of(count):
            part = other.at[h, pl.ds(s, count), pl.ds(0, n_peers)]
            return remote(part, part, send2.at[h, s], recv2.at[h, s], (peers[0], my_ta))

        @pl.when((n < paired) & (n % ROUND == 0))
        def _():
            act(of(ROUND))

        @pl.when(n >= paired)
        def _():
            act(of(1))

    def couple(n, carry):
        h, s = n // pair_count, n % pair_count

        @pl.when(n >= LAG)
        def _():
            flows((n - LAG) // pair_count, (n - LAG) % pair_count)

        arrival(n, lambda copy: copy.wait_recv())
        index = n
        for m in range(modes):
            row = window[s, pl.ds(number(s, MODE + m), 1), :]
            scale = jnp.broadcast_to(row, (TILE, trans)).astype(jnp.bfloat16)
            for t in range(tiles):
                block = other[h, s, t].reshape(half // TILE, TILE, LANES)
                block = block * scale[None, :, t * LANES:(t + 1) * LANES]
                scaled[m * half:(m + 1) * half, t * LANES:(t + 1) * LANES] = block.reshape(half, LANES)
        product = lax.dot_general(
            scaled[...], held[number(s, PLACE)],
            (((1,), (1,)), ((), ())), preferred_element_type=jnp.float32,
        ).reshape(modes, ta_count, strip, rows)
        for q in range(ta_count):
            part = jnp.concatenate(
                [product[:, q].reshape(modes * strip, rows), jnp.zeros((pad, rows), jnp.float32)], axis=0
            )
            part_out[index, q] = part.astype(jnp.bfloat16)
        for mate in mates:
            remote(
                part_out.at[index, mate], part_in.at[index, my_ta],
                send3.at[index], recv3.at[index], (my_pb, mate),
            ).start()
        part_in[index, my_ta] = part_out[index, my_ta]
        return carry

    lax.fori_loop(0, HALVES * pair_count, couple, 0)
    for s in range(pair_count - LAG, pair_count):
        flows(HALVES - 1, s)

    used = 2 * HALVES * strip
    stacked = jnp.concatenate(
        [acc_first[...].reshape(used, rows), jnp.zeros((LANES - used, rows), jnp.float32)], axis=0
    )
    first_out[...] = jnp.transpose(stacked)
    for peer in far_peers:
        remote(
            first_out.at[pl.ds(pl.multiple_of(peer * blocks, blocks), blocks)], first_in.at[my_pb],
            send4.at[0], recv4.at[0], (peer, my_ta),
        ).start()
    for mate in mates:
        remote(acc_second, second_in.at[my_ta], send4.at[1], recv4.at[1], (my_pb, mate)).start()
    first_in[my_pb] = first_out[pl.ds(pl.multiple_of(my_pb * blocks, blocks), blocks)]
    second_in[my_ta] = acc_second[...]

    for h in range(HALVES):
        for k, peer in enumerate(peers):
            lane = pl.multiple_of(peer * LANES, LANES)
            remote(
                coeffs.at[:, pl.ds(h * half, half), pl.ds(lane, LANES)],
                pieces[h].at[pl.ds(my_pb * blocks, blocks)],
                send1.at[h, k], recv1.at[h, k], (peer, my_ta),
            ).wait_send()

    def sent(n, carry):
        arrival(n, lambda copy: copy.wait_send())
        block = part_in.at[n, pl.ds(0, n_mates)]
        remote(block, block, send3.at[n], recv3.at[n], (my_pb, mates[0])).wait_send()
        return carry

    lax.fori_loop(0, HALVES * pair_count, sent, 0)

    few = first_in.at[pl.ds(0, n_peers)]
    sums = remote(few, few, send4.at[0], recv4.at[0], (peers[0], my_ta))
    sums.wait_recv()
    total[...] = jnp.sum(first_in[...], axis=0)
    for mate in mates:
        remote(total, total_in.at[my_ta], send4.at[2], recv4.at[2], (my_pb, mate)).start()
    total_in[my_ta] = total[...]
    sums.wait_send()
    for ref, sem in ((second_in, 1), (total_in, 2)):
        few = ref.at[pl.ds(0, n_mates)]
        copy = remote(few, few, send4.at[sem], recv4.at[sem], (my_pb, mates[0]))
        copy.wait_send()
        copy.wait_recv()
    lane = lax.broadcasted_iota(jnp.int32, (blocks, LANES), 1)
    for c in range(2):
        flow = jnp.sum(second_in[:, c], axis=0)
        for h in range(HALVES):
            low = (c * HALVES + h) * strip
            inside = (lane >= low) & (lane < low + strip)
            for q in range(ta_count):
                target = h * half + q * strip
                part = jnp.where(inside, total_in[q], 0.0)
                flow = flow + pltpu.roll(part, (target - low) % LANES, 1)
        flow_out[c] = flow


def shards(
    coeffs,
    elph_table,
    energies,
    phonon_energy,
    deviation,
    source,
    inv_tau,
    block_pairs,
    mode_index,
    offsets,
):
    blocks, rows, trans = coeffs.shape
    modes, trans_all = elph_table.shape
    pair_total = block_pairs.shape[0]
    pb_count = lax.axis_size("pb")
    ta_count = lax.axis_size("ta")
    half = rows // HALVES
    strip = half // ta_count
    units = HALVES * PAIRS_DEV
    padded = -(-modes * strip // TILE) * TILE
    list_lanes = -(-pair_total // LANES) * LANES
    smem = pl.BlockSpec(memory_space=pltpu.SMEM)
    vmem = pl.BlockSpec(memory_space=pltpu.VMEM)
    f32, bf16 = jnp.float32, jnp.bfloat16
    dma = pltpu.SemaphoreType.DMA
    flow = pl.pallas_call(
        kernel,
        out_shape=pltpu.VMEM((2, blocks, rows), f32),
        in_specs=[smem, pl.BlockSpec(memory_space=pl.ANY)] + [vmem] * 6,
        out_specs=vmem,
        scratch_shapes=[
            pltpu.VMEM((blocks, rows, trans), bf16),
            pltpu.VMEM((pb_count * blocks, half, LANES), bf16),
            pltpu.VMEM((pb_count * blocks, half, LANES), bf16),
            pltpu.VMEM((HALVES, PAIRS_DEV, pb_count - 1, half, LANES), bf16),
            pltpu.VMEM((HALVES, PAIRS_DEV, pb_count, half, LANES), bf16),
            pltpu.VMEM((modes * half, trans), bf16),
            pltpu.VMEM((units, ta_count, padded, rows), bf16),
            pltpu.VMEM((units, ta_count, padded, rows), bf16),
            pltpu.VMEM((PAIRS_DEV, HALVES, modes, strip, rows), f32),
            pltpu.VMEM((PAIRS_DEV, HALVES, modes, strip, rows), f32),
            pltpu.VMEM((PAIRS_DEV, HALVES, strip, rows), f32),
            pltpu.VMEM(((trans_all + trans) // LANES + 1, TILE, LANES), f32),
            pltpu.VMEM((PAIRS_DEV, TILE, trans), f32),
            pltpu.VMEM((rows, rows), f32),
            pltpu.VMEM((LANES, list_lanes), jnp.int32),
            pltpu.SMEM((TILE, list_lanes), jnp.int32),
            pltpu.VMEM((2, HALVES, strip, rows), f32),
            pltpu.VMEM((2, blocks, rows), f32),
            pltpu.VMEM((pb_count * blocks, LANES), f32),
            pltpu.VMEM((pb_count, blocks, LANES), f32),
            pltpu.VMEM((ta_count, 2, blocks, rows), f32),
            pltpu.VMEM((blocks, LANES), f32),
            pltpu.VMEM((ta_count, blocks, LANES), f32),
            dma((2,)),
            dma((HALVES, pb_count - 1)), dma((HALVES, pb_count - 1)),
            dma((HALVES, PAIRS_DEV)), dma((HALVES, PAIRS_DEV)),
            dma((units,)), dma((units,)),
            dma((3,)), dma((3,)),
        ],
        compiler_params=pltpu.CompilerParams(
            collective_id=0, has_side_effects=True, vmem_limit_bytes=56 << 20
        ),
        name="rates",
    )(
        phonon_energy, coeffs, elph_table, energies, deviation, block_pairs.T, mode_index.T,
        offsets.reshape(1, pair_total),
    )
    return (source + flow[1]) / (inv_tau + flow[0]), flow[0]


def solution(mesh):
    in_specs = (
        P("pb", None, "ta"),
        P(),
        P(),
        P(),
        P(),
        P("pb", None),
        P("pb", None),
        P(),
        P(),
        P(),
    )
    out_specs = (P("pb", None), P("pb", None))
    return jax.shard_map(shards, mesh=mesh, in_specs=in_specs, out_specs=out_specs, check_vma=False)
```

```python
import jax
import jax.numpy as jnp
from jax import lax
from jax.experimental import pallas as pl
from jax.experimental.pallas import tpu as pltpu
from jax.sharding import PartitionSpec as P

PAIRS_DEV = 12
BOLTZMANN_KT = 0.02585
BROADENING = 0.01
MESH = pl.DeviceIdType.MESH
LANES = 128
TILE = 16
HALVES = 2
ROUND = 2
SINGLE = 4
LAG = 4
FIRST, SECOND, PLACE, START, SHIFT, SWAPPED, MODE = range(7)

SIDE = 4
KINDS = 2
COPIES = 2
SPREAD = (
    (1, 0, 0), (0, 1, 0), (3, 0, 1), (0, 3, 0), (1, 1, 0), (0, 2, 0), (3, 3, 1),
    (0, 1, 1), (1, 3, 0), (0, 3, 1), (3, 1, 1), (1, 2, 0), (0, 2, 1), (3, 2, 1),
)
GIVE = (
    (1, 0, 1), (0, 1, 0), (3, 0, 0), (0, 3, 0), (1, 1, 1), (0, 2, 0), (3, 3, 0),
    (0, 1, 1), (1, 3, 1), (0, 3, 1), (3, 1, 0), (1, 2, 1), (0, 2, 1), (3, 2, 0),
)
FAR_MOVES = (
    (2, 2), (2, 1), (1, 2), (2, 3), (3, 2), (1, 1), (3, 3), (1, 3),
    (3, 1), (2, 0), (0, 2), (1, 0), (0, 1), (3, 0), (0, 3),
)
MATES = (4, 3, 5, 2, 6, 1, 7)


def kernel(
    phonon, coeffs, table, energies, deviation, block_pairs, mode_index, offsets,
    flow_out,
    held, pieces_a, pieces_b, stage, other, scaled, part_out, part_in,
    weight_f, weight_b, value_a, wide, window, turn, lists, ints,
    acc_first, acc_second, first_out, first_in, second_in, total, total_in,
    local, send1, recv1, send2, recv2, send3, recv3, send4, recv4, send5, recv5,
):
    blocks, rows, trans = coeffs.shape
    modes, trans_all = table.shape
    pair_total = block_pairs.shape[1]
    pair_count = other.shape[2]
    paired = HALVES * pair_count - SINGLE
    my_pb = lax.axis_index("pb")
    my_ta = lax.axis_index("ta")
    ta_count = part_in.shape[1]
    half = rows // HALVES
    strip = half // ta_count
    my_y, my_z = my_pb // SIDE, my_pb % SIDE
    places = (my_y, my_z)
    share = half // KINDS
    far_peers = [((my_y + dy) % 4) * 4 + (my_z + dz) % 4 for dy, dz in FAR_MOVES]
    mates = [(my_ta + d) % ta_count for d in MATES]
    n_peers, n_mates = len(far_peers), len(mates)
    pieces = (pieces_a, pieces_b)

    barrier = pltpu.get_barrier_semaphore()
    for peer in far_peers:
        pl.semaphore_signal(barrier, inc=1, device_id=(peer, my_ta), device_id_type=MESH)
    for mate in mates:
        pl.semaphore_signal(barrier, inc=1, device_id=(my_pb, mate), device_id_type=MESH)
    fetch = pltpu.make_async_copy(coeffs, held, local.at[0])
    fetch.start()
    pl.semaphore_wait(barrier, n_peers + n_mates)

    def remote(src, dst, send, recv, device):
        return pltpu.make_async_remote_copy(
            src_ref=src, dst_ref=dst, send_sem=send, recv_sem=recv,
            device_id=device, device_id_type=MESH,
        )

    def coords(t):
        return places[t], places[1 - t]

    def device(t, main, side):
        return main * SIDE + side if t == 0 else side * SIDE + main

    def lane_of(t, main, side):
        return pl.ds(pl.multiple_of(device(t, main, side) * LANES, LANES), LANES)

    def blocks_of(main, side):
        return pl.ds((main * SIDE + side) * blocks, blocks)

    def rows_of(h, t):
        return pl.ds(h * half + t * share, share)

    def back(place, copy):
        return (place + SIDE - copy) % SIDE

    for h in range(HALVES):
        for first, second, copy in SPREAD:
            for t in range(KINDS):
                main, side = coords(t)
                to_main, to_side = (main + first) % SIDE, (side + second) % SIDE
                remote(
                    coeffs.at[:, rows_of(h, t), lane_of(t, back(to_main, copy), to_side)],
                    pieces[h].at[t, copy, blocks_of(main, side)],
                    send1.at[h, t], recv1.at[h, t], (device(t, to_main, to_side), my_ta),
                ).start()

    shift_of = blocks.bit_length() - 1
    spread_lanes = lists.shape[1]
    lists[...] = jnp.zeros_like(lists)
    lists[0:2, 0:pair_total] = block_pairs[...]
    lists[2:3, 0:pair_total] = offsets[...]
    lists[MODE:MODE + modes, 0:pair_total] = mode_index[...]
    column_form = jnp.transpose(lists[...])[:pair_total]
    second = column_form[:, 1:2]
    owner = lax.shift_right_logical(second, shift_of)
    serial = lax.broadcasted_iota(jnp.int32, (pair_total, LANES), 0)
    mine = (lax.broadcasted_iota(jnp.int32, (pair_total, LANES), 1) == owner).astype(jnp.int32)
    count = mine
    step = 1
    while step < pair_total:
        count = count + jnp.where(serial >= step, pltpu.roll(count, step, 0), 0)
        step *= 2
    rank = jnp.sum(mine * (count - 1), axis=1, keepdims=True)
    slot = owner * pair_count + rank
    hot = lax.broadcasted_iota(jnp.int32, (pair_total, spread_lanes), 1) == slot
    start = column_form[:, 2:3] + my_ta * trans
    start = jnp.where(start >= trans_all, start - trans_all, start)

    def swap(block):
        owner_of = lax.shift_right_logical(block, shift_of)
        swapped = (owner_of & (SIDE - 1)) * SIDE + lax.shift_right_logical(owner_of, SIDE.bit_length() - 1)
        return swapped * blocks + (block & (blocks - 1))

    columns = [
        column_form[:, 0:1], second, second & (blocks - 1),
        lax.shift_right_logical(start, 7), start & (LANES - 1),
        swap(column_form[:, 0:1]),
    ] + [column_form[:, MODE + m:MODE + m + 1] for m in range(modes)]
    for c, column in enumerate(columns):
        lists[c:c + 1, :] = jnp.sum(jnp.where(hot, column, 0), axis=0, keepdims=True)
    listing = pltpu.make_async_copy(lists.at[pl.ds(0, TILE)], ints, local.at[1])
    listing.start()
    fetch.wait()
    listing.wait()
    for h in range(HALVES):
        for t in range(KINDS):
            main, side = coords(t)
            for copy in range(COPIES):
                pieces[h][t, copy, blocks_of(main, side)] = held[:, rows_of(h, t), lane_of(t, back(main, copy), side)]

    def number(s, which):
        return ints[which, my_pb * pair_count + s]

    def spread_of(h, t):
        part = stage.at[h, t, pl.ds(0, blocks)]
        return remote(part, part, send1.at[h, t], recv1.at[h, t], (far_peers[0], my_ta))

    def copies_of(h, t):
        part = pieces[h].at[t, 0]
        return remote(part, part, send5.at[h, t], recv5.at[h, t], (far_peers[0], my_ta))

    def hand_on(h):
        for t in range(KINDS):
            spread_of(h, t).wait_recv()
        for w in range(SIDE):
            for t in range(KINDS):
                main, side = coords(t)
                for copy, move in ((0, 1), (1, SIDE - 1)):
                    to = (main + move) % SIDE
                    for origin in (main, (main + SIDE - move) % SIDE):
                        remote(
                            pieces[h].at[t, copy, blocks_of(origin, w)], pieces[h].at[t, 1 - copy, blocks_of(origin, w)],
                            send5.at[h, t], recv5.at[h, t], (device(t, to, side), my_ta),
                        ).start()

    def give_out(h):
        for t in range(KINDS):
            copies_of(h, t).wait_recv()

        def piece(t, copy, place, s):
            return pieces[h][t, copy, ints[SWAPPED if t else FIRST, place * pair_count + s]]

        def deliver(s, count):
            for k, (first, second, copy) in enumerate(GIVE):
                for t in range(KINDS):
                    main, side = coords(t)
                    to = device(t, (main + first) % SIDE, (side + second) % SIDE)
                    for u in range(count):
                        stage[h, t, s + u, k] = piece(t, copy, to, s + u)
                    remote(
                        stage.at[h, t, pl.ds(s, count), k],
                        other.at[h, t, pl.ds(s, count), device(t, back(main, copy), side)],
                        send2.at[h, t, s], recv2.at[h, t, s], (to, my_ta),
                    ).start()
            for t in range(KINDS):
                main, side = coords(t)
                for copy in range(COPIES):
                    for u in range(count):
                        other[h, t, s + u, device(t, back(main, copy), side)] = piece(t, copy, my_pb, s + u)

        def deliver_round(g, carry):
            deliver(ROUND * g, ROUND)
            return carry

        def deliver_one(s, carry):
            deliver(s, 1)
            return carry

        singles = SINGLE if h == HALVES - 1 else 0
        lax.fori_loop(0, (pair_count - singles) // ROUND, deliver_round, 0)
        lax.fori_loop(pair_count - singles, pair_count, deliver_one, 0)

    for h in range(HALVES):
        hand_on(h)
    give_out(0)

    wide[...] = jnp.zeros_like(wide)
    tiles_all = trans_all // LANES
    tiles = trans // LANES

    def widen(tile, carry):
        lane = pl.multiple_of(lax.rem(tile, tiles_all) * LANES, LANES)
        wide[tile, pl.ds(0, modes), :] = table[:, pl.ds(lane, LANES)].astype(jnp.float32)
        return carry

    lax.fori_loop(0, wide.shape[0], widen, 0)
    acc_first[...] = jnp.zeros_like(acc_first)
    acc_second[...] = jnp.zeros_like(acc_second)

    def strips_of(source_ref, block):
        row = source_ref[pl.ds(block, 1), :]
        turn[...] = jnp.transpose(jnp.broadcast_to(row, (rows, rows)))
        return [
            turn[pl.ds(pl.multiple_of(h * half + my_ta * strip, strip), strip), :]
            for h in range(HALVES)
        ]

    def prepare(s, carry):
        first, second_one = number(s, FIRST), number(s, SECOND)
        piece = wide[pl.ds(number(s, START), tiles + 1)]
        amount = jnp.full(piece.shape, number(s, SHIFT), jnp.int32)
        for bit in range(7):
            moved = pltpu.roll(piece, LANES - (1 << bit), 2)
            piece = jnp.where((amount & (1 << bit)) != 0, moved, piece)
        keep = lax.broadcasted_iota(jnp.int32, (TILE, LANES), 1) < LANES - amount[0]
        for t in range(tiles):
            window[s, :, t * LANES:(t + 1) * LANES] = jnp.where(keep, piece[t], piece[t + 1])
        energy_b = energies[pl.ds(second_one, 1), :]
        energy_a = strips_of(energies, first)
        for h in range(HALVES):
            detuning = energy_a[h] - energy_b
            for m in range(modes):
                energy = jnp.full(detuning.shape, phonon[m], jnp.float32)
                bose = 1.0 / (jnp.exp(energy / BOLTZMANN_KT) - 1.0)
                minus = 1.0 / (1.0 + ((detuning - energy) / BROADENING) ** 2)
                plus = 1.0 / (1.0 + ((detuning + energy) / BROADENING) ** 2)
                scale = 1.0 / (modes * rows)
                weight_f[s, h, m] = ((bose + 1.0) * minus + bose * plus) * scale
                weight_b[s, h, m] = ((bose + 1.0) * plus + bose * minus) * scale
        for h, value in enumerate(strips_of(deviation, first)):
            value_a[s, h] = value
        return carry

    lax.fori_loop(0, pair_count, prepare, 0)
    for h in range(1, HALVES):
        give_out(h)

    def flows(h, s):
        index = h * pair_count + s
        copy = remote(
            part_in.at[index, pl.ds(0, n_mates)], part_in.at[index, pl.ds(0, n_mates)],
            send3.at[index], recv3.at[index], (my_pb, mates[0]),
        )
        copy.wait_recv()
        coupling = part_in[index, 0].astype(jnp.float32)
        for q in range(1, ta_count):
            coupling = coupling + part_in[index, q].astype(jnp.float32)
        coupling = coupling[:modes * strip].reshape(modes, strip, rows)
        square = coupling * coupling
        forward = jnp.sum(square * weight_f[s, h], axis=0)
        backward = jnp.sum(square * weight_b[s, h], axis=0)
        value_b = deviation[pl.ds(number(s, SECOND), 1), :]
        out_first = jnp.sum(forward, axis=1, keepdims=True)
        in_first = jnp.sum(backward * value_b, axis=1, keepdims=True)
        out_second = jnp.sum(backward, axis=0, keepdims=True)
        in_second = jnp.sum(forward * value_a[s, h], axis=0, keepdims=True)
        here = lax.broadcasted_iota(jnp.int32, (strip, rows), 1) == number(s, FIRST)
        acc_first[0, h] += jnp.where(here, out_first, 0.0)
        acc_first[1, h] += jnp.where(here, in_first, 0.0)
        there = lax.broadcasted_iota(jnp.int32, (blocks, rows), 0) == number(s, PLACE)
        acc_second[0] += jnp.where(there, out_second, 0.0)
        acc_second[1] += jnp.where(there, in_second, 0.0)

    pad = part_out.shape[2] - modes * strip

    def arrival(n, act):
        h, s = n // pair_count, n % pair_count

        def of(t, count):
            part = stage.at[h, t, pl.ds(s, count)]
            return remote(part, part, send2.at[h, t, s], recv2.at[h, t, s], (far_peers[0], my_ta))

        @pl.when((n < paired) & (n % ROUND == 0))
        def _():
            for t in range(KINDS):
                act(of(t, ROUND))

        @pl.when(n >= paired)
        def _():
            for t in range(KINDS):
                act(of(t, 1))

    def couple(n, carry):
        h, s = n // pair_count, n % pair_count

        @pl.when(n >= LAG)
        def _():
            flows((n - LAG) // pair_count, (n - LAG) % pair_count)

        arrival(n, lambda copy: copy.wait_recv())
        index = n
        for m in range(modes):
            row = window[s, pl.ds(number(s, MODE + m), 1), :]
            scale = jnp.broadcast_to(row, (TILE, trans)).astype(jnp.bfloat16)
            for t in range(tiles):
                for kind in range(KINDS):
                    block = other[h, kind, s, t].reshape(share // TILE, TILE, LANES)
                    block = block * scale[None, :, t * LANES:(t + 1) * LANES]
                    low = m * half + kind * share
                    scaled[low:low + share, t * LANES:(t + 1) * LANES] = block.reshape(share, LANES)
        product = lax.dot_general(
            scaled[...], held[number(s, PLACE)],
            (((1,), (1,)), ((), ())), preferred_element_type=jnp.float32,
        ).reshape(modes, ta_count, strip, rows)
        for q in range(ta_count):
            part = jnp.concatenate(
                [product[:, q].reshape(modes * strip, rows), jnp.zeros((pad, rows), jnp.float32)], axis=0
            )
            part_out[index, q] = part.astype(jnp.bfloat16)
        for mate in mates:
            remote(
                part_out.at[index, mate], part_in.at[index, my_ta],
                send3.at[index], recv3.at[index], (my_pb, mate),
            ).start()
        part_in[index, my_ta] = part_out[index, my_ta]
        return carry

    lax.fori_loop(0, HALVES * pair_count, couple, 0)
    for s in range(pair_count - LAG, pair_count):
        flows(HALVES - 1, s)

    used = 2 * HALVES * strip
    stacked = jnp.concatenate(
        [acc_first[...].reshape(used, rows), jnp.zeros((LANES - used, rows), jnp.float32)], axis=0
    )
    first_out[...] = jnp.transpose(stacked)
    for peer in far_peers:
        remote(
            first_out.at[pl.ds(pl.multiple_of(peer * blocks, blocks), blocks)], first_in.at[my_pb],
            send4.at[0], recv4.at[0], (peer, my_ta),
        ).start()
    for mate in mates:
        remote(acc_second, second_in.at[my_ta], send4.at[1], recv4.at[1], (my_pb, mate)).start()
    first_in[my_pb] = first_out[pl.ds(pl.multiple_of(my_pb * blocks, blocks), blocks)]
    second_in[my_ta] = acc_second[...]

    for h in range(HALVES):
        for t in range(KINDS):
            spread_of(h, t).wait_send()
            copies_of(h, t).wait_send()

    def sent(n, carry):
        arrival(n, lambda copy: copy.wait_send())
        block = part_in.at[n, pl.ds(0, n_mates)]
        remote(block, block, send3.at[n], recv3.at[n], (my_pb, mates[0])).wait_send()
        return carry

    lax.fori_loop(0, HALVES * pair_count, sent, 0)

    few = first_in.at[pl.ds(0, n_peers)]
    sums = remote(few, few, send4.at[0], recv4.at[0], (far_peers[0], my_ta))
    sums.wait_recv()
    total[...] = jnp.sum(first_in[...], axis=0)
    for mate in mates:
        remote(total, total_in.at[my_ta], send4.at[2], recv4.at[2], (my_pb, mate)).start()
    total_in[my_ta] = total[...]
    sums.wait_send()
    for ref, sem in ((second_in, 1), (total_in, 2)):
        few = ref.at[pl.ds(0, n_mates)]
        copy = remote(few, few, send4.at[sem], recv4.at[sem], (my_pb, mates[0]))
        copy.wait_send()
        copy.wait_recv()
    lane = lax.broadcasted_iota(jnp.int32, (blocks, LANES), 1)
    for c in range(2):
        flow = jnp.sum(second_in[:, c], axis=0)
        for h in range(HALVES):
            low = (c * HALVES + h) * strip
            inside = (lane >= low) & (lane < low + strip)
            for q in range(ta_count):
                target = h * half + q * strip
                part = jnp.where(inside, total_in[q], 0.0)
                flow = flow + pltpu.roll(part, (target - low) % LANES, 1)
        flow_out[c] = flow


def shards(
    coeffs,
    elph_table,
    energies,
    phonon_energy,
    deviation,
    source,
    inv_tau,
    block_pairs,
    mode_index,
    offsets,
):
    blocks, rows, trans = coeffs.shape
    modes, trans_all = elph_table.shape
    pair_total = block_pairs.shape[0]
    pb_count = lax.axis_size("pb")
    ta_count = lax.axis_size("ta")
    half = rows // HALVES
    share = half // KINDS
    strip = half // ta_count
    units = HALVES * PAIRS_DEV
    padded = -(-modes * strip // TILE) * TILE
    list_lanes = -(-pair_total // LANES) * LANES
    smem = pl.BlockSpec(memory_space=pltpu.SMEM)
    vmem = pl.BlockSpec(memory_space=pltpu.VMEM)
    f32, bf16 = jnp.float32, jnp.bfloat16
    dma = pltpu.SemaphoreType.DMA
    flow = pl.pallas_call(
        kernel,
        out_shape=pltpu.VMEM((2, blocks, rows), f32),
        in_specs=[smem, pl.BlockSpec(memory_space=pl.ANY)] + [vmem] * 6,
        out_specs=vmem,
        scratch_shapes=[
            pltpu.VMEM((blocks, rows, trans), bf16),
            pltpu.VMEM((KINDS, COPIES, pb_count * blocks, share, LANES), bf16),
            pltpu.VMEM((KINDS, COPIES, pb_count * blocks, share, LANES), bf16),
            pltpu.VMEM((HALVES, KINDS, PAIRS_DEV, len(GIVE), share, LANES), bf16),
            pltpu.VMEM((HALVES, KINDS, PAIRS_DEV, pb_count, share, LANES), bf16),
            pltpu.VMEM((modes * half, trans), bf16),
            pltpu.VMEM((units, ta_count, padded, rows), bf16),
            pltpu.VMEM((units, ta_count, padded, rows), bf16),
            pltpu.VMEM((PAIRS_DEV, HALVES, modes, strip, rows), f32),
            pltpu.VMEM((PAIRS_DEV, HALVES, modes, strip, rows), f32),
            pltpu.VMEM((PAIRS_DEV, HALVES, strip, rows), f32),
            pltpu.VMEM(((trans_all + trans) // LANES + 1, TILE, LANES), f32),
            pltpu.VMEM((PAIRS_DEV, TILE, trans), f32),
            pltpu.VMEM((rows, rows), f32),
            pltpu.VMEM((LANES, list_lanes), jnp.int32),
            pltpu.SMEM((TILE, list_lanes), jnp.int32),
            pltpu.VMEM((2, HALVES, strip, rows), f32),
            pltpu.VMEM((2, blocks, rows), f32),
            pltpu.VMEM((pb_count * blocks, LANES), f32),
            pltpu.VMEM((pb_count, blocks, LANES), f32),
            pltpu.VMEM((ta_count, 2, blocks, rows), f32),
            pltpu.VMEM((blocks, LANES), f32),
            pltpu.VMEM((ta_count, blocks, LANES), f32),
            dma((2,)),
            dma((HALVES, KINDS)), dma((HALVES, KINDS)),
            dma((HALVES, KINDS, PAIRS_DEV)), dma((HALVES, KINDS, PAIRS_DEV)),
            dma((units,)), dma((units,)),
            dma((3,)), dma((3,)),
            dma((HALVES, KINDS)), dma((HALVES, KINDS)),
        ],
        compiler_params=pltpu.CompilerParams(
            collective_id=0, has_side_effects=True, vmem_limit_bytes=56 << 20
        ),
        name="rates",
    )(
        phonon_energy, coeffs, elph_table, energies, deviation, block_pairs.T, mode_index.T,
        offsets.reshape(1, pair_total),
    )
    return (source + flow[1]) / (inv_tau + flow[0]), flow[0]


def solution(mesh):
    in_specs = (
        P("pb", None, "ta"),
        P(),
        P(),
        P(),
        P(),
        P("pb", None),
        P("pb", None),
        P(),
        P(),
        P(),
    )
    out_specs = (P("pb", None), P("pb", None))
    return jax.shard_map(shards, mesh=mesh, in_specs=in_specs, out_specs=out_specs, check_vma=False)
```

```python
import jax
import jax.numpy as jnp
from jax import lax
from jax.experimental import pallas as pl
from jax.experimental.pallas import tpu as pltpu
from jax.sharding import PartitionSpec as P

PAIRS_DEV = 12
BOLTZMANN_KT = 0.02585
BROADENING = 0.01
MESH = pl.DeviceIdType.MESH
LANES = 128
TILE = 16
HALVES = 2
ROUND = 2
SINGLE = 8
LAG = 4
FIRST, SECOND, PLACE, START, SHIFT, SWAPPED, MODE = range(7)

SIDE = 4
BATCH = 4
KINDS = 2
COPIES = 2
SPREAD = (
    (1, 0, 0), (0, 1, 0), (3, 0, 1), (0, 3, 0), (1, 1, 0), (0, 2, 0), (3, 3, 1),
    (0, 1, 1), (1, 3, 0), (0, 3, 1), (3, 1, 1), (1, 2, 0), (0, 2, 1), (3, 2, 1),
)
GIVE = (
    (1, 0, 1), (0, 1, 0), (3, 0, 0), (0, 3, 0), (1, 1, 1), (0, 2, 0), (3, 3, 0),
    (0, 1, 1), (1, 3, 1), (0, 3, 1), (3, 1, 0), (1, 2, 1), (0, 2, 1), (3, 2, 0),
)
FAR_MOVES = (
    (2, 2), (2, 1), (1, 2), (2, 3), (3, 2), (1, 1), (3, 3), (1, 3),
    (3, 1), (2, 0), (0, 2), (1, 0), (0, 1), (3, 0), (0, 3),
)
MATES = (4, 3, 5, 2, 6, 1, 7)


def kernel(
    phonon, coeffs, table, energies, deviation, block_pairs, mode_index, offsets,
    flow_out,
    held, pieces_a, pieces_b, stage, other, scaled, part_out, part_in,
    weight_f, weight_b, value_a, wide, window, turn, lists, ints,
    acc_first, acc_second, first_out, first_in, second_in, total, total_in,
    local, send1, recv1, send2, recv2, send3, recv3, send4, recv4, send5, recv5,
):
    blocks, rows, trans = coeffs.shape
    modes, trans_all = table.shape
    pair_total = block_pairs.shape[1]
    pair_count = other.shape[2]
    paired = HALVES * pair_count - SINGLE
    my_pb = lax.axis_index("pb")
    my_ta = lax.axis_index("ta")
    ta_count = part_in.shape[1]
    half = rows // HALVES
    strip = half // ta_count
    my_y, my_z = my_pb // SIDE, my_pb % SIDE
    places = (my_y, my_z)
    share = half // KINDS
    far_peers = [((my_y + dy) % 4) * 4 + (my_z + dz) % 4 for dy, dz in FAR_MOVES]
    mates = [(my_ta + d) % ta_count for d in MATES]
    n_peers, n_mates = len(far_peers), len(mates)
    pieces = (pieces_a, pieces_b)

    barrier = pltpu.get_barrier_semaphore()
    for peer in far_peers:
        pl.semaphore_signal(barrier, inc=1, device_id=(peer, my_ta), device_id_type=MESH)
    for mate in mates:
        pl.semaphore_signal(barrier, inc=1, device_id=(my_pb, mate), device_id_type=MESH)
    fetch = pltpu.make_async_copy(coeffs, held, local.at[0])
    fetch.start()
    pl.semaphore_wait(barrier, n_peers + n_mates)

    def remote(src, dst, send, recv, device):
        return pltpu.make_async_remote_copy(
            src_ref=src, dst_ref=dst, send_sem=send, recv_sem=recv,
            device_id=device, device_id_type=MESH,
        )

    def coords(t):
        return places[t], places[1 - t]

    def device(t, main, side):
        return main * SIDE + side if t == 0 else side * SIDE + main

    def lane_of(t, main, side):
        return pl.ds(pl.multiple_of(device(t, main, side) * LANES, LANES), LANES)

    def blocks_of(main, side):
        return pl.ds((main * SIDE + side) * blocks, blocks)

    def rows_of(h, t):
        return pl.ds(h * half + t * share, share)

    def back(place, copy):
        return (place + SIDE - copy) % SIDE

    for h, part in [(h, part) for h in range(HALVES) for part in range(0, blocks, BATCH)]:
        for first, second, copy in SPREAD:
            for t in range(KINDS):
                main, side = coords(t)
                to_main, to_side = (main + first) % SIDE, (side + second) % SIDE
                remote(
                    coeffs.at[pl.ds(part, BATCH), rows_of(h, t), lane_of(t, back(to_main, copy), to_side)],
                    pieces[h].at[t, copy, pl.ds((main * SIDE + side) * blocks + part, BATCH)],
                    send1.at[h, t], recv1.at[h, t], (device(t, to_main, to_side), my_ta),
                ).start()

    shift_of = blocks.bit_length() - 1
    spread_lanes = lists.shape[1]
    lists[...] = jnp.zeros_like(lists)
    lists[0:2, 0:pair_total] = block_pairs[...]
    lists[2:3, 0:pair_total] = offsets[...]
    lists[MODE:MODE + modes, 0:pair_total] = mode_index[...]
    column_form = jnp.transpose(lists[...])[:pair_total]
    second = column_form[:, 1:2]
    owner = lax.shift_right_logical(second, shift_of)
    serial = lax.broadcasted_iota(jnp.int32, (pair_total, LANES), 0)
    mine = (lax.broadcasted_iota(jnp.int32, (pair_total, LANES), 1) == owner).astype(jnp.int32)
    count = mine
    step = 1
    while step < pair_total:
        count = count + jnp.where(serial >= step, pltpu.roll(count, step, 0), 0)
        step *= 2
    rank = jnp.sum(mine * (count - 1), axis=1, keepdims=True)
    slot = owner * pair_count + rank
    hot = lax.broadcasted_iota(jnp.int32, (pair_total, spread_lanes), 1) == slot
    start = column_form[:, 2:3] + my_ta * trans
    start = jnp.where(start >= trans_all, start - trans_all, start)

    def swap(block):
        owner_of = lax.shift_right_logical(block, shift_of)
        swapped = (owner_of & (SIDE - 1)) * SIDE + lax.shift_right_logical(owner_of, SIDE.bit_length() - 1)
        return swapped * blocks + (block & (blocks - 1))

    columns = [
        column_form[:, 0:1], second, second & (blocks - 1),
        lax.shift_right_logical(start, 7), start & (LANES - 1),
        swap(column_form[:, 0:1]),
    ] + [column_form[:, MODE + m:MODE + m + 1] for m in range(modes)]
    for c, column in enumerate(columns):
        lists[c:c + 1, :] = jnp.sum(jnp.where(hot, column, 0), axis=0, keepdims=True)
    listing = pltpu.make_async_copy(lists.at[pl.ds(0, TILE)], ints, local.at[1])
    listing.start()
    fetch.wait()
    listing.wait()
    for h in range(HALVES):
        for t in range(KINDS):
            main, side = coords(t)
            for copy in range(COPIES):
                pieces[h][t, copy, blocks_of(main, side)] = held[:, rows_of(h, t), lane_of(t, back(main, copy), side)]

    def number(s, which):
        return ints[which, my_pb * pair_count + s]

    def spread_of(h, t):
        part = stage.at[h, t, pl.ds(0, blocks)]
        return remote(part, part, send1.at[h, t], recv1.at[h, t], (far_peers[0], my_ta))

    def copies_of(h, t):
        part = pieces[h].at[t, 0]
        return remote(part, part, send5.at[h, t], recv5.at[h, t], (far_peers[0], my_ta))

    def hand_on(h):
        for t in range(KINDS):
            spread_of(h, t).wait_recv()
        for w in range(SIDE):
            for t in range(KINDS):
                main, side = coords(t)
                for copy, move in ((0, 1), (1, SIDE - 1)):
                    to = (main + move) % SIDE
                    for origin in (main, (main + SIDE - move) % SIDE):
                        remote(
                            pieces[h].at[t, copy, blocks_of(origin, w)], pieces[h].at[t, 1 - copy, blocks_of(origin, w)],
                            send5.at[h, t], recv5.at[h, t], (device(t, to, side), my_ta),
                        ).start()

    def give_out(h):
        for t in range(KINDS):
            copies_of(h, t).wait_recv()

        def piece(t, copy, place, s):
            return pieces[h][t, copy, ints[SWAPPED if t else FIRST, place * pair_count + s]]

        def deliver(s, count):
            for k, (first, second, copy) in enumerate(GIVE):
                for t in range(KINDS):
                    main, side = coords(t)
                    to = device(t, (main + first) % SIDE, (side + second) % SIDE)
                    for u in range(count):
                        stage[h, t, s + u, k] = piece(t, copy, to, s + u)
                    remote(
                        stage.at[h, t, pl.ds(s, count), k],
                        other.at[h, t, pl.ds(s, count), device(t, back(main, copy), side)],
                        send2.at[h, t, s], recv2.at[h, t, s], (to, my_ta),
                    ).start()
            for t in range(KINDS):
                main, side = coords(t)
                for copy in range(COPIES):
                    for u in range(count):
                        other[h, t, s + u, device(t, back(main, copy), side)] = piece(t, copy, my_pb, s + u)

        def deliver_round(g, carry):
            deliver(ROUND * g, ROUND)
            return carry

        def deliver_one(s, carry):
            deliver(s, 1)
            return carry

        singles = SINGLE if h == HALVES - 1 else 0
        lax.fori_loop(0, (pair_count - singles) // ROUND, deliver_round, 0)
        lax.fori_loop(pair_count - singles, pair_count, deliver_one, 0)

    for h in range(HALVES):
        hand_on(h)
    give_out(0)

    wide[...] = jnp.zeros_like(wide)
    tiles_all = trans_all // LANES
    tiles = trans // LANES

    def widen(tile, carry):
        lane = pl.multiple_of(lax.rem(tile, tiles_all) * LANES, LANES)
        wide[tile, pl.ds(0, modes), :] = table[:, pl.ds(lane, LANES)].astype(jnp.float32)
        return carry

    lax.fori_loop(0, wide.shape[0], widen, 0)
    acc_first[...] = jnp.zeros_like(acc_first)
    acc_second[...] = jnp.zeros_like(acc_second)

    def strips_of(source_ref, block):
        row = source_ref[pl.ds(block, 1), :]
        turn[...] = jnp.transpose(jnp.broadcast_to(row, (rows, rows)))
        return [
            turn[pl.ds(pl.multiple_of(h * half + my_ta * strip, strip), strip), :]
            for h in range(HALVES)
        ]

    def prepare(s, carry):
        first, second_one = number(s, FIRST), number(s, SECOND)
        piece = wide[pl.ds(number(s, START), tiles + 1)]
        amount = jnp.full(piece.shape, number(s, SHIFT), jnp.int32)
        for bit in range(7):
            moved = pltpu.roll(piece, LANES - (1 << bit), 2)
            piece = jnp.where((amount & (1 << bit)) != 0, moved, piece)
        keep = lax.broadcasted_iota(jnp.int32, (TILE, LANES), 1) < LANES - amount[0]
        for t in range(tiles):
            window[s, :, t * LANES:(t + 1) * LANES] = jnp.where(keep, piece[t], piece[t + 1])
        energy_b = energies[pl.ds(second_one, 1), :]
        energy_a = strips_of(energies, first)
        for h in range(HALVES):
            detuning = energy_a[h] - energy_b
            for m in range(modes):
                energy = jnp.full(detuning.shape, phonon[m], jnp.float32)
                bose = 1.0 / (jnp.exp(energy / BOLTZMANN_KT) - 1.0)
                minus = 1.0 / (1.0 + ((detuning - energy) / BROADENING) ** 2)
                plus = 1.0 / (1.0 + ((detuning + energy) / BROADENING) ** 2)
                scale = 1.0 / (modes * rows)
                weight_f[s, h, m] = ((bose + 1.0) * minus + bose * plus) * scale
                weight_b[s, h, m] = ((bose + 1.0) * plus + bose * minus) * scale
        for h, value in enumerate(strips_of(deviation, first)):
            value_a[s, h] = value
        return carry

    lax.fori_loop(0, pair_count, prepare, 0)
    for h in range(1, HALVES):
        give_out(h)

    def flows(h, s):
        index = h * pair_count + s
        copy = remote(
            part_in.at[index, pl.ds(0, n_mates)], part_in.at[index, pl.ds(0, n_mates)],
            send3.at[index], recv3.at[index], (my_pb, mates[0]),
        )
        copy.wait_recv()
        coupling = part_in[index, 0].astype(jnp.float32)
        for q in range(1, ta_count):
            coupling = coupling + part_in[index, q].astype(jnp.float32)
        coupling = coupling[:modes * strip].reshape(modes, strip, rows)
        square = coupling * coupling
        forward = jnp.sum(square * weight_f[s, h], axis=0)
        backward = jnp.sum(square * weight_b[s, h], axis=0)
        value_b = deviation[pl.ds(number(s, SECOND), 1), :]
        out_first = jnp.sum(forward, axis=1, keepdims=True)
        in_first = jnp.sum(backward * value_b, axis=1, keepdims=True)
        out_second = jnp.sum(backward, axis=0, keepdims=True)
        in_second = jnp.sum(forward * value_a[s, h], axis=0, keepdims=True)
        here = lax.broadcasted_iota(jnp.int32, (strip, rows), 1) == number(s, FIRST)
        acc_first[0, h] += jnp.where(here, out_first, 0.0)
        acc_first[1, h] += jnp.where(here, in_first, 0.0)
        there = lax.broadcasted_iota(jnp.int32, (blocks, rows), 0) == number(s, PLACE)
        acc_second[0] += jnp.where(there, out_second, 0.0)
        acc_second[1] += jnp.where(there, in_second, 0.0)

    pad = part_out.shape[2] - modes * strip

    def arrival(n, act):
        h, s = n // pair_count, n % pair_count

        def of(t, count):
            part = stage.at[h, t, pl.ds(s, count)]
            return remote(part, part, send2.at[h, t, s], recv2.at[h, t, s], (far_peers[0], my_ta))

        @pl.when((n < paired) & (n % ROUND == 0))
        def _():
            for t in range(KINDS):
                act(of(t, ROUND))

        @pl.when(n >= paired)
        def _():
            for t in range(KINDS):
                act(of(t, 1))

    def couple(n, carry):
        h, s = n // pair_count, n % pair_count

        @pl.when(n >= LAG)
        def _():
            flows((n - LAG) // pair_count, (n - LAG) % pair_count)

        arrival(n, lambda copy: copy.wait_recv())
        index = n
        for m in range(modes):
            row = window[s, pl.ds(number(s, MODE + m), 1), :]
            scale = jnp.broadcast_to(row, (TILE, trans)).astype(jnp.bfloat16)
            for t in range(tiles):
                for kind in range(KINDS):
                    block = other[h, kind, s, t].reshape(share // TILE, TILE, LANES)
                    block = block * scale[None, :, t * LANES:(t + 1) * LANES]
                    low = m * half + kind * share
                    scaled[low:low + share, t * LANES:(t + 1) * LANES] = block.reshape(share, LANES)
        product = lax.dot_general(
            scaled[...], held[number(s, PLACE)],
            (((1,), (1,)), ((), ())), preferred_element_type=jnp.float32,
        ).reshape(modes, ta_count, strip, rows)
        for q in range(ta_count):
            part = jnp.concatenate(
                [product[:, q].reshape(modes * strip, rows), jnp.zeros((pad, rows), jnp.float32)], axis=0
            )
            part_out[index, q] = part.astype(jnp.bfloat16)
        for mate in mates:
            remote(
                part_out.at[index, mate], part_in.at[index, my_ta],
                send3.at[index], recv3.at[index], (my_pb, mate),
            ).start()
        part_in[index, my_ta] = part_out[index, my_ta]
        return carry

    lax.fori_loop(0, HALVES * pair_count, couple, 0)
    for s in range(pair_count - LAG, pair_count):
        flows(HALVES - 1, s)

    used = 2 * HALVES * strip
    stacked = jnp.concatenate(
        [acc_first[...].reshape(used, rows), jnp.zeros((LANES - used, rows), jnp.float32)], axis=0
    )
    first_out[...] = jnp.transpose(stacked)
    for peer in far_peers:
        remote(
            first_out.at[pl.ds(pl.multiple_of(peer * blocks, blocks), blocks)], first_in.at[my_pb],
            send4.at[0], recv4.at[0], (peer, my_ta),
        ).start()
    for mate in mates:
        remote(acc_second, second_in.at[my_ta], send4.at[1], recv4.at[1], (my_pb, mate)).start()
    first_in[my_pb] = first_out[pl.ds(pl.multiple_of(my_pb * blocks, blocks), blocks)]
    second_in[my_ta] = acc_second[...]

    for h in range(HALVES):
        for t in range(KINDS):
            spread_of(h, t).wait_send()
            copies_of(h, t).wait_send()

    def sent(n, carry):
        arrival(n, lambda copy: copy.wait_send())
        block = part_in.at[n, pl.ds(0, n_mates)]
        remote(block, block, send3.at[n], recv3.at[n], (my_pb, mates[0])).wait_send()
        return carry

    lax.fori_loop(0, HALVES * pair_count, sent, 0)

    few = first_in.at[pl.ds(0, n_peers)]
    sums = remote(few, few, send4.at[0], recv4.at[0], (far_peers[0], my_ta))
    sums.wait_recv()
    total[...] = jnp.sum(first_in[...], axis=0)
    for mate in mates:
        remote(total, total_in.at[my_ta], send4.at[2], recv4.at[2], (my_pb, mate)).start()
    total_in[my_ta] = total[...]
    sums.wait_send()
    for ref, sem in ((second_in, 1), (total_in, 2)):
        few = ref.at[pl.ds(0, n_mates)]
        copy = remote(few, few, send4.at[sem], recv4.at[sem], (my_pb, mates[0]))
        copy.wait_send()
        copy.wait_recv()
    lane = lax.broadcasted_iota(jnp.int32, (blocks, LANES), 1)
    for c in range(2):
        flow = jnp.sum(second_in[:, c], axis=0)
        for h in range(HALVES):
            low = (c * HALVES + h) * strip
            inside = (lane >= low) & (lane < low + strip)
            for q in range(ta_count):
                target = h * half + q * strip
                part = jnp.where(inside, total_in[q], 0.0)
                flow = flow + pltpu.roll(part, (target - low) % LANES, 1)
        flow_out[c] = flow


def shards(
    coeffs,
    elph_table,
    energies,
    phonon_energy,
    deviation,
    source,
    inv_tau,
    block_pairs,
    mode_index,
    offsets,
):
    blocks, rows, trans = coeffs.shape
    modes, trans_all = elph_table.shape
    pair_total = block_pairs.shape[0]
    pb_count = lax.axis_size("pb")
    ta_count = lax.axis_size("ta")
    half = rows // HALVES
    share = half // KINDS
    strip = half // ta_count
    units = HALVES * PAIRS_DEV
    padded = -(-modes * strip // TILE) * TILE
    list_lanes = -(-pair_total // LANES) * LANES
    smem = pl.BlockSpec(memory_space=pltpu.SMEM)
    vmem = pl.BlockSpec(memory_space=pltpu.VMEM)
    f32, bf16 = jnp.float32, jnp.bfloat16
    dma = pltpu.SemaphoreType.DMA
    flow = pl.pallas_call(
        kernel,
        out_shape=pltpu.VMEM((2, blocks, rows), f32),
        in_specs=[smem, pl.BlockSpec(memory_space=pl.ANY)] + [vmem] * 6,
        out_specs=vmem,
        scratch_shapes=[
            pltpu.VMEM((blocks, rows, trans), bf16),
            pltpu.VMEM((KINDS, COPIES, pb_count * blocks, share, LANES), bf16),
            pltpu.VMEM((KINDS, COPIES, pb_count * blocks, share, LANES), bf16),
            pltpu.VMEM((HALVES, KINDS, PAIRS_DEV, len(GIVE), share, LANES), bf16),
            pltpu.VMEM((HALVES, KINDS, PAIRS_DEV, pb_count, share, LANES), bf16),
            pltpu.VMEM((modes * half, trans), bf16),
            pltpu.VMEM((units, ta_count, padded, rows), bf16),
            pltpu.VMEM((units, ta_count, padded, rows), bf16),
            pltpu.VMEM((PAIRS_DEV, HALVES, modes, strip, rows), f32),
            pltpu.VMEM((PAIRS_DEV, HALVES, modes, strip, rows), f32),
            pltpu.VMEM((PAIRS_DEV, HALVES, strip, rows), f32),
            pltpu.VMEM(((trans_all + trans) // LANES + 1, TILE, LANES), f32),
            pltpu.VMEM((PAIRS_DEV, TILE, trans), f32),
            pltpu.VMEM((rows, rows), f32),
            pltpu.VMEM((LANES, list_lanes), jnp.int32),
            pltpu.SMEM((TILE, list_lanes), jnp.int32),
            pltpu.VMEM((2, HALVES, strip, rows), f32),
            pltpu.VMEM((2, blocks, rows), f32),
            pltpu.VMEM((pb_count * blocks, LANES), f32),
            pltpu.VMEM((pb_count, blocks, LANES), f32),
            pltpu.VMEM((ta_count, 2, blocks, rows), f32),
            pltpu.VMEM((blocks, LANES), f32),
            pltpu.VMEM((ta_count, blocks, LANES), f32),
            dma((2,)),
            dma((HALVES, KINDS)), dma((HALVES, KINDS)),
            dma((HALVES, KINDS, PAIRS_DEV)), dma((HALVES, KINDS, PAIRS_DEV)),
            dma((units,)), dma((units,)),
            dma((3,)), dma((3,)),
            dma((HALVES, KINDS)), dma((HALVES, KINDS)),
        ],
        compiler_params=pltpu.CompilerParams(
            collective_id=0, has_side_effects=True, vmem_limit_bytes=56 << 20
        ),
        name="rates",
    )(
        phonon_energy, coeffs, elph_table, energies, deviation, block_pairs.T, mode_index.T,
        offsets.reshape(1, pair_total),
    )
    return (source + flow[1]) / (inv_tau + flow[0]), flow[0]


def solution(mesh):
    in_specs = (
        P("pb", None, "ta"),
        P(),
        P(),
        P(),
        P(),
        P("pb", None),
        P("pb", None),
        P(),
        P(),
        P(),
    )
    out_specs = (P("pb", None), P("pb", None))
    return jax.shard_map(shards, mesh=mesh, in_specs=in_specs, out_specs=out_specs, check_vma=False)
```

```python
import jax
import jax.numpy as jnp
from jax import lax
from jax.experimental import pallas as pl
from jax.experimental.pallas import tpu as pltpu
from jax.sharding import PartitionSpec as P

PAIRS_DEV = 12
BOLTZMANN_KT = 0.02585
BROADENING = 0.01
MESH = pl.DeviceIdType.MESH
LANES = 128
TILE = 16
HALVES = 2
ROUND = 2
SINGLE = 8
LAG = 4
FIRST, SECOND, PLACE, START, SHIFT, SWAPPED, MODE = range(7)

SIDE = 4
BATCH = 4
KINDS = 2
COPIES = 2
SPREAD = (
    (1, 0, 0), (0, 1, 0), (3, 0, 1), (0, 3, 0), (1, 1, 0), (0, 2, 0), (3, 3, 1),
    (0, 1, 1), (1, 3, 0), (0, 3, 1), (3, 1, 1), (1, 2, 0), (0, 2, 1), (3, 2, 1),
)
GIVE = (
    (1, 0, 1), (0, 1, 0), (3, 2, 0), (0, 3, 1), (1, 1, 1), (3, 0, 0), (0, 2, 0),
    (1, 3, 1), (0, 1, 1), (3, 3, 0), (0, 3, 0), (1, 2, 1), (3, 1, 0), (0, 2, 1),
)
FAR_MOVES = (
    (2, 2), (2, 1), (1, 2), (2, 3), (3, 2), (1, 1), (3, 3), (1, 3),
    (3, 1), (2, 0), (0, 2), (1, 0), (0, 1), (3, 0), (0, 3),
)
MATES = (4, 3, 5, 2, 6, 1, 7)


def kernel(
    phonon, coeffs, table, energies, deviation, block_pairs, mode_index, offsets,
    flow_out,
    held, pieces_a, pieces_b, stage, other, scaled, part_out, part_in,
    weight_f, weight_b, value_a, wide, window, turn, lists, ints,
    acc_first, acc_second, first_out, first_in, second_in, total, total_in,
    local, send1, recv1, send2, recv2, send3, recv3, send4, recv4, send5, recv5,
):
    blocks, rows, trans = coeffs.shape
    modes, trans_all = table.shape
    pair_total = block_pairs.shape[1]
    pair_count = other.shape[2]
    paired = HALVES * pair_count - SINGLE
    my_pb = lax.axis_index("pb")
    my_ta = lax.axis_index("ta")
    ta_count = part_in.shape[1]
    half = rows // HALVES
    strip = half // ta_count
    my_y, my_z = my_pb // SIDE, my_pb % SIDE
    places = (my_y, my_z)
    share = half // KINDS
    far_peers = [((my_y + dy) % 4) * 4 + (my_z + dz) % 4 for dy, dz in FAR_MOVES]
    mates = [(my_ta + d) % ta_count for d in MATES]
    n_peers, n_mates = len(far_peers), len(mates)
    pieces = (pieces_a, pieces_b)

    barrier = pltpu.get_barrier_semaphore()
    for peer in far_peers:
        pl.semaphore_signal(barrier, inc=1, device_id=(peer, my_ta), device_id_type=MESH)
    for mate in mates:
        pl.semaphore_signal(barrier, inc=1, device_id=(my_pb, mate), device_id_type=MESH)
    fetch = pltpu.make_async_copy(coeffs, held, local.at[0])
    fetch.start()
    pl.semaphore_wait(barrier, n_peers + n_mates)

    def remote(src, dst, send, recv, device):
        return pltpu.make_async_remote_copy(
            src_ref=src, dst_ref=dst, send_sem=send, recv_sem=recv,
            device_id=device, device_id_type=MESH,
        )

    def coords(t):
        return places[t], places[1 - t]

    def device(t, main, side):
        return main * SIDE + side if t == 0 else side * SIDE + main

    def lane_of(t, main, side):
        return pl.ds(pl.multiple_of(device(t, main, side) * LANES, LANES), LANES)

    def blocks_of(main, side):
        return pl.ds((main * SIDE + side) * blocks, blocks)

    def rows_of(h, t):
        return pl.ds(h * half + t * share, share)

    def back(place, copy):
        return (place + SIDE - copy) % SIDE

    for h, part in [(h, part) for h in range(HALVES) for part in range(0, blocks, BATCH)]:
        for first, second, copy in SPREAD:
            for t in range(KINDS):
                main, side = coords(t)
                to_main, to_side = (main + first) % SIDE, (side + second) % SIDE
                remote(
                    coeffs.at[pl.ds(part, BATCH), rows_of(h, t), lane_of(t, back(to_main, copy), to_side)],
                    pieces[h].at[t, copy, pl.ds((main * SIDE + side) * blocks + part, BATCH)],
                    send1.at[h, t], recv1.at[h, t], (device(t, to_main, to_side), my_ta),
                ).start()

    shift_of = blocks.bit_length() - 1
    spread_lanes = lists.shape[1]
    lists[...] = jnp.zeros_like(lists)
    lists[0:2, 0:pair_total] = block_pairs[...]
    lists[2:3, 0:pair_total] = offsets[...]
    lists[MODE:MODE + modes, 0:pair_total] = mode_index[...]
    column_form = jnp.transpose(lists[...])[:pair_total]
    second = column_form[:, 1:2]
    owner = lax.shift_right_logical(second, shift_of)
    serial = lax.broadcasted_iota(jnp.int32, (pair_total, LANES), 0)
    mine = (lax.broadcasted_iota(jnp.int32, (pair_total, LANES), 1) == owner).astype(jnp.int32)
    count = mine
    step = 1
    while step < pair_total:
        count = count + jnp.where(serial >= step, pltpu.roll(count, step, 0), 0)
        step *= 2
    rank = jnp.sum(mine * (count - 1), axis=1, keepdims=True)
    slot = owner * pair_count + rank
    hot = lax.broadcasted_iota(jnp.int32, (pair_total, spread_lanes), 1) == slot
    start = column_form[:, 2:3] + my_ta * trans
    start = jnp.where(start >= trans_all, start - trans_all, start)

    def swap(block):
        owner_of = lax.shift_right_logical(block, shift_of)
        swapped = (owner_of & (SIDE - 1)) * SIDE + lax.shift_right_logical(owner_of, SIDE.bit_length() - 1)
        return swapped * blocks + (block & (blocks - 1))

    columns = [
        column_form[:, 0:1], second, second & (blocks - 1),
        lax.shift_right_logical(start, 7), start & (LANES - 1),
        swap(column_form[:, 0:1]),
    ] + [column_form[:, MODE + m:MODE + m + 1] for m in range(modes)]
    for c, column in enumerate(columns):
        lists[c:c + 1, :] = jnp.sum(jnp.where(hot, column, 0), axis=0, keepdims=True)
    listing = pltpu.make_async_copy(lists.at[pl.ds(0, TILE)], ints, local.at[1])
    listing.start()
    fetch.wait()
    listing.wait()
    for h in range(HALVES):
        for t in range(KINDS):
            main, side = coords(t)
            for copy in range(COPIES):
                pieces[h][t, copy, blocks_of(main, side)] = held[:, rows_of(h, t), lane_of(t, back(main, copy), side)]

    def number(s, which):
        return ints[which, my_pb * pair_count + s]

    def spread_of(h, t):
        part = stage.at[h, t, pl.ds(0, blocks)]
        return remote(part, part, send1.at[h, t], recv1.at[h, t], (far_peers[0], my_ta))

    def copies_of(h, t):
        part = pieces[h].at[t, 0]
        return remote(part, part, send5.at[h, t], recv5.at[h, t], (far_peers[0], my_ta))

    def hand_on(h):
        for t in range(KINDS):
            spread_of(h, t).wait_recv()
        for w in range(SIDE):
            for t in range(KINDS):
                main, side = coords(t)
                for copy, move in ((0, 1), (1, SIDE - 1)):
                    to = (main + move) % SIDE
                    for origin in (main, (main + SIDE - move) % SIDE):
                        remote(
                            pieces[h].at[t, copy, blocks_of(origin, w)], pieces[h].at[t, 1 - copy, blocks_of(origin, w)],
                            send5.at[h, t], recv5.at[h, t], (device(t, to, side), my_ta),
                        ).start()

    def give_out(h):
        for t in range(KINDS):
            copies_of(h, t).wait_recv()

        def piece(t, copy, place, s):
            return pieces[h][t, copy, ints[SWAPPED if t else FIRST, place * pair_count + s]]

        def deliver(s, count):
            for k, (first, second, copy) in enumerate(GIVE):
                for t in range(KINDS):
                    main, side = coords(t)
                    to = device(t, (main + first) % SIDE, (side + second) % SIDE)
                    for u in range(count):
                        stage[h, t, s + u, k] = piece(t, copy, to, s + u)
                    remote(
                        stage.at[h, t, pl.ds(s, count), k],
                        other.at[h, t, pl.ds(s, count), device(t, back(main, copy), side)],
                        send2.at[h, t, s], recv2.at[h, t, s], (to, my_ta),
                    ).start()
            for t in range(KINDS):
                main, side = coords(t)
                for copy in range(COPIES):
                    for u in range(count):
                        other[h, t, s + u, device(t, back(main, copy), side)] = piece(t, copy, my_pb, s + u)

        def deliver_round(g, carry):
            deliver(ROUND * g, ROUND)
            return carry

        def deliver_one(s, carry):
            deliver(s, 1)
            return carry

        singles = SINGLE if h == HALVES - 1 else 0
        lax.fori_loop(0, (pair_count - singles) // ROUND, deliver_round, 0)
        lax.fori_loop(pair_count - singles, pair_count, deliver_one, 0)

    for h in range(HALVES):
        hand_on(h)
    give_out(0)

    wide[...] = jnp.zeros_like(wide)
    tiles_all = trans_all // LANES
    tiles = trans // LANES

    def widen(tile, carry):
        lane = pl.multiple_of(lax.rem(tile, tiles_all) * LANES, LANES)
        wide[tile, pl.ds(0, modes), :] = table[:, pl.ds(lane, LANES)].astype(jnp.float32)
        return carry

    lax.fori_loop(0, wide.shape[0], widen, 0)
    acc_first[...] = jnp.zeros_like(acc_first)
    acc_second[...] = jnp.zeros_like(acc_second)

    def strips_of(source_ref, block):
        row = source_ref[pl.ds(block, 1), :]
        turn[...] = jnp.transpose(jnp.broadcast_to(row, (rows, rows)))
        return [
            turn[pl.ds(pl.multiple_of(h * half + my_ta * strip, strip), strip), :]
            for h in range(HALVES)
        ]

    def prepare(s, carry):
        first, second_one = number(s, FIRST), number(s, SECOND)
        piece = wide[pl.ds(number(s, START), tiles + 1)]
        amount = jnp.full(piece.shape, number(s, SHIFT), jnp.int32)
        for bit in range(7):
            moved = pltpu.roll(piece, LANES - (1 << bit), 2)
            piece = jnp.where((amount & (1 << bit)) != 0, moved, piece)
        keep = lax.broadcasted_iota(jnp.int32, (TILE, LANES), 1) < LANES - amount[0]
        for t in range(tiles):
            window[s, :, t * LANES:(t + 1) * LANES] = jnp.where(keep, piece[t], piece[t + 1])
        energy_b = energies[pl.ds(second_one, 1), :]
        energy_a = strips_of(energies, first)
        for h in range(HALVES):
            detuning = energy_a[h] - energy_b
            for m in range(modes):
                energy = jnp.full(detuning.shape, phonon[m], jnp.float32)
                bose = 1.0 / (jnp.exp(energy / BOLTZMANN_KT) - 1.0)
                minus = 1.0 / (1.0 + ((detuning - energy) / BROADENING) ** 2)
                plus = 1.0 / (1.0 + ((detuning + energy) / BROADENING) ** 2)
                scale = 1.0 / (modes * rows)
                weight_f[s, h, m] = ((bose + 1.0) * minus + bose * plus) * scale
                weight_b[s, h, m] = ((bose + 1.0) * plus + bose * minus) * scale
        for h, value in enumerate(strips_of(deviation, first)):
            value_a[s, h] = value
        return carry

    lax.fori_loop(0, pair_count, prepare, 0)
    for h in range(1, HALVES):
        give_out(h)

    def flows(h, s):
        index = h * pair_count + s
        copy = remote(
            part_in.at[index, pl.ds(0, n_mates)], part_in.at[index, pl.ds(0, n_mates)],
            send3.at[index], recv3.at[index], (my_pb, mates[0]),
        )
        copy.wait_recv()
        coupling = part_in[index, 0].astype(jnp.float32)
        for q in range(1, ta_count):
            coupling = coupling + part_in[index, q].astype(jnp.float32)
        coupling = coupling[:modes * strip].reshape(modes, strip, rows)
        square = coupling * coupling
        forward = jnp.sum(square * weight_f[s, h], axis=0)
        backward = jnp.sum(square * weight_b[s, h], axis=0)
        value_b = deviation[pl.ds(number(s, SECOND), 1), :]
        out_first = jnp.sum(forward, axis=1, keepdims=True)
        in_first = jnp.sum(backward * value_b, axis=1, keepdims=True)
        out_second = jnp.sum(backward, axis=0, keepdims=True)
        in_second = jnp.sum(forward * value_a[s, h], axis=0, keepdims=True)
        here = lax.broadcasted_iota(jnp.int32, (strip, rows), 1) == number(s, FIRST)
        acc_first[0, h] += jnp.where(here, out_first, 0.0)
        acc_first[1, h] += jnp.where(here, in_first, 0.0)
        there = lax.broadcasted_iota(jnp.int32, (blocks, rows), 0) == number(s, PLACE)
        acc_second[0] += jnp.where(there, out_second, 0.0)
        acc_second[1] += jnp.where(there, in_second, 0.0)

    pad = part_out.shape[2] - modes * strip

    def arrival(n, act):
        h, s = n // pair_count, n % pair_count

        def of(t, count):
            part = stage.at[h, t, pl.ds(s, count)]
            return remote(part, part, send2.at[h, t, s], recv2.at[h, t, s], (far_peers[0], my_ta))

        @pl.when((n < paired) & (n % ROUND == 0))
        def _():
            for t in range(KINDS):
                act(of(t, ROUND))

        @pl.when(n >= paired)
        def _():
            for t in range(KINDS):
                act(of(t, 1))

    def couple(n, carry):
        h, s = n // pair_count, n % pair_count

        @pl.when(n >= LAG)
        def _():
            flows((n - LAG) // pair_count, (n - LAG) % pair_count)

        arrival(n, lambda copy: copy.wait_recv())
        index = n
        for m in range(modes):
            row = window[s, pl.ds(number(s, MODE + m), 1), :]
            scale = jnp.broadcast_to(row, (TILE, trans)).astype(jnp.bfloat16)
            for t in range(tiles):
                for kind in range(KINDS):
                    block = other[h, kind, s, t].reshape(share // TILE, TILE, LANES)
                    block = block * scale[None, :, t * LANES:(t + 1) * LANES]
                    low = m * half + kind * share
                    scaled[low:low + share, t * LANES:(t + 1) * LANES] = block.reshape(share, LANES)
        product = lax.dot_general(
            scaled[...], held[number(s, PLACE)],
            (((1,), (1,)), ((), ())), preferred_element_type=jnp.float32,
        ).reshape(modes, ta_count, strip, rows)
        for q in range(ta_count):
            part = jnp.concatenate(
                [product[:, q].reshape(modes * strip, rows), jnp.zeros((pad, rows), jnp.float32)], axis=0
            )
            part_out[index, q] = part.astype(jnp.bfloat16)
        for mate in mates:
            remote(
                part_out.at[index, mate], part_in.at[index, my_ta],
                send3.at[index], recv3.at[index], (my_pb, mate),
            ).start()
        part_in[index, my_ta] = part_out[index, my_ta]
        return carry

    lax.fori_loop(0, HALVES * pair_count, couple, 0)
    for s in range(pair_count - LAG, pair_count):
        flows(HALVES - 1, s)

    used = 2 * HALVES * strip
    stacked = jnp.concatenate(
        [acc_first[...].reshape(used, rows), jnp.zeros((LANES - used, rows), jnp.float32)], axis=0
    )
    first_out[...] = jnp.transpose(stacked)
    for peer in far_peers:
        remote(
            first_out.at[pl.ds(pl.multiple_of(peer * blocks, blocks), blocks)], first_in.at[my_pb],
            send4.at[0], recv4.at[0], (peer, my_ta),
        ).start()
    for mate in mates:
        remote(acc_second, second_in.at[my_ta], send4.at[1], recv4.at[1], (my_pb, mate)).start()
    first_in[my_pb] = first_out[pl.ds(pl.multiple_of(my_pb * blocks, blocks), blocks)]
    second_in[my_ta] = acc_second[...]

    for h in range(HALVES):
        for t in range(KINDS):
            spread_of(h, t).wait_send()
            copies_of(h, t).wait_send()

    def sent(n, carry):
        arrival(n, lambda copy: copy.wait_send())
        block = part_in.at[n, pl.ds(0, n_mates)]
        remote(block, block, send3.at[n], recv3.at[n], (my_pb, mates[0])).wait_send()
        return carry

    lax.fori_loop(0, pair_count, sent, 0)

    few = first_in.at[pl.ds(0, n_peers)]
    sums = remote(few, few, send4.at[0], recv4.at[0], (far_peers[0], my_ta))
    sums.wait_recv()
    total[...] = jnp.sum(first_in[...], axis=0)
    for mate in mates:
        remote(total, total_in.at[my_ta], send4.at[2], recv4.at[2], (my_pb, mate)).start()
    total_in[my_ta] = total[...]
    lax.fori_loop(pair_count, HALVES * pair_count, sent, 0)
    sums.wait_send()
    for ref, sem in ((second_in, 1), (total_in, 2)):
        few = ref.at[pl.ds(0, n_mates)]
        copy = remote(few, few, send4.at[sem], recv4.at[sem], (my_pb, mates[0]))
        copy.wait_send()
        copy.wait_recv()
    lane = lax.broadcasted_iota(jnp.int32, (blocks, LANES), 1)
    for c in range(2):
        flow = jnp.sum(second_in[:, c], axis=0)
        for h in range(HALVES):
            low = (c * HALVES + h) * strip
            inside = (lane >= low) & (lane < low + strip)
            for q in range(ta_count):
                target = h * half + q * strip
                part = jnp.where(inside, total_in[q], 0.0)
                flow = flow + pltpu.roll(part, (target - low) % LANES, 1)
        flow_out[c] = flow


def shards(
    coeffs,
    elph_table,
    energies,
    phonon_energy,
    deviation,
    source,
    inv_tau,
    block_pairs,
    mode_index,
    offsets,
):
    blocks, rows, trans = coeffs.shape
    modes, trans_all = elph_table.shape
    pair_total = block_pairs.shape[0]
    pb_count = lax.axis_size("pb")
    ta_count = lax.axis_size("ta")
    half = rows // HALVES
    share = half // KINDS
    strip = half // ta_count
    units = HALVES * PAIRS_DEV
    padded = -(-modes * strip // TILE) * TILE
    list_lanes = -(-pair_total // LANES) * LANES
    smem = pl.BlockSpec(memory_space=pltpu.SMEM)
    vmem = pl.BlockSpec(memory_space=pltpu.VMEM)
    f32, bf16 = jnp.float32, jnp.bfloat16
    dma = pltpu.SemaphoreType.DMA
    flow = pl.pallas_call(
        kernel,
        out_shape=pltpu.VMEM((2, blocks, rows), f32),
        in_specs=[smem, pl.BlockSpec(memory_space=pl.ANY)] + [vmem] * 6,
        out_specs=vmem,
        scratch_shapes=[
            pltpu.VMEM((blocks, rows, trans), bf16),
            pltpu.VMEM((KINDS, COPIES, pb_count * blocks, share, LANES), bf16),
            pltpu.VMEM((KINDS, COPIES, pb_count * blocks, share, LANES), bf16),
            pltpu.VMEM((HALVES, KINDS, PAIRS_DEV, len(GIVE), share, LANES), bf16),
            pltpu.VMEM((HALVES, KINDS, PAIRS_DEV, pb_count, share, LANES), bf16),
            pltpu.VMEM((modes * half, trans), bf16),
            pltpu.VMEM((units, ta_count, padded, rows), bf16),
            pltpu.VMEM((units, ta_count, padded, rows), bf16),
            pltpu.VMEM((PAIRS_DEV, HALVES, modes, strip, rows), f32),
            pltpu.VMEM((PAIRS_DEV, HALVES, modes, strip, rows), f32),
            pltpu.VMEM((PAIRS_DEV, HALVES, strip, rows), f32),
            pltpu.VMEM(((trans_all + trans) // LANES + 1, TILE, LANES), f32),
            pltpu.VMEM((PAIRS_DEV, TILE, trans), f32),
            pltpu.VMEM((rows, rows), f32),
            pltpu.VMEM((LANES, list_lanes), jnp.int32),
            pltpu.SMEM((TILE, list_lanes), jnp.int32),
            pltpu.VMEM((2, HALVES, strip, rows), f32),
            pltpu.VMEM((2, blocks, rows), f32),
            pltpu.VMEM((pb_count * blocks, LANES), f32),
            pltpu.VMEM((pb_count, blocks, LANES), f32),
            pltpu.VMEM((ta_count, 2, blocks, rows), f32),
            pltpu.VMEM((blocks, LANES), f32),
            pltpu.VMEM((ta_count, blocks, LANES), f32),
            dma((2,)),
            dma((HALVES, KINDS)), dma((HALVES, KINDS)),
            dma((HALVES, KINDS, PAIRS_DEV)), dma((HALVES, KINDS, PAIRS_DEV)),
            dma((units,)), dma((units,)),
            dma((3,)), dma((3,)),
            dma((HALVES, KINDS)), dma((HALVES, KINDS)),
        ],
        compiler_params=pltpu.CompilerParams(
            collective_id=0, has_side_effects=True, vmem_limit_bytes=56 << 20
        ),
        name="rates",
    )(
        phonon_energy, coeffs, elph_table, energies, deviation, block_pairs.T, mode_index.T,
        offsets.reshape(1, pair_total),
    )
    return (source + flow[1]) / (inv_tau + flow[0]), flow[0]


def solution(mesh):
    in_specs = (
        P("pb", None, "ta"),
        P(),
        P(),
        P(),
        P(),
        P("pb", None),
        P("pb", None),
        P(),
        P(),
        P(),
    )
    out_specs = (P("pb", None), P("pb", None))
    return jax.shard_map(shards, mesh=mesh, in_specs=in_specs, out_specs=out_specs, check_vma=False)
```

```python
import jax
import jax.numpy as jnp
from jax import lax
from jax.experimental import pallas as pl
from jax.experimental.pallas import tpu as pltpu
from jax.sharding import PartitionSpec as P

PAIRS_DEV = 12
BOLTZMANN_KT = 0.02585
BROADENING = 0.01
MESH = pl.DeviceIdType.MESH
LANES = 128
TILE = 16
HALVES = 2
ROUND = 2
SINGLE = 8
LAG = 4
FIRST, SECOND, PLACE, START, SHIFT, SWAPPED, MODE = range(7)

SIDE = 4
BATCH = 4
KINDS = 2
COPIES = 2
SPREAD = (
    (1, 0, 0), (0, 1, 0), (3, 2, 1), (0, 3, 1), (1, 1, 0), (3, 0, 1), (0, 2, 0),
    (1, 3, 0), (0, 1, 1), (3, 3, 1), (0, 3, 0), (1, 2, 0), (3, 1, 1), (0, 2, 1),
)
GIVE = (
    (1, 0, 1), (0, 1, 0), (3, 2, 0), (0, 3, 1), (1, 1, 1), (3, 0, 0), (0, 2, 0),
    (1, 3, 1), (0, 1, 1), (3, 3, 0), (0, 3, 0), (1, 2, 1), (3, 1, 0), (0, 2, 1),
)
FAR_MOVES = (
    (2, 2), (2, 1), (1, 2), (2, 3), (3, 2), (1, 1), (3, 3), (1, 3),
    (3, 1), (2, 0), (0, 2), (1, 0), (0, 1), (3, 0), (0, 3),
)
MATES = (4, 3, 5, 2, 6, 1, 7)


def kernel(
    phonon, coeffs, table, energies, deviation, block_pairs, mode_index, offsets,
    flow_out,
    held, pieces_a, pieces_b, stage, other, scaled, part_out, part_in,
    weight_f, weight_b, value_a, wide, window, turn, lists, ints,
    acc_first, acc_second, first_out, first_in, second_in, total, total_in,
    local, send1, recv1, send2, recv2, send3, recv3, send4, recv4, send5, recv5,
):
    blocks, rows, trans = coeffs.shape
    modes, trans_all = table.shape
    pair_total = block_pairs.shape[1]
    pair_count = other.shape[2]
    paired = HALVES * pair_count - SINGLE
    my_pb = lax.axis_index("pb")
    my_ta = lax.axis_index("ta")
    ta_count = part_in.shape[1]
    half = rows // HALVES
    strip = half // ta_count
    my_y, my_z = my_pb // SIDE, my_pb % SIDE
    places = (my_y, my_z)
    share = half // KINDS
    far_peers = [((my_y + dy) % 4) * 4 + (my_z + dz) % 4 for dy, dz in FAR_MOVES]
    mates = [(my_ta + d) % ta_count for d in MATES]
    n_peers, n_mates = len(far_peers), len(mates)
    pieces = (pieces_a, pieces_b)

    barrier = pltpu.get_barrier_semaphore()
    for peer in far_peers:
        pl.semaphore_signal(barrier, inc=1, device_id=(peer, my_ta), device_id_type=MESH)
    for mate in mates:
        pl.semaphore_signal(barrier, inc=1, device_id=(my_pb, mate), device_id_type=MESH)
    fetch = pltpu.make_async_copy(coeffs, held, local.at[0])
    fetch.start()
    pl.semaphore_wait(barrier, n_peers + n_mates)

    def remote(src, dst, send, recv, device):
        return pltpu.make_async_remote_copy(
            src_ref=src, dst_ref=dst, send_sem=send, recv_sem=recv,
            device_id=device, device_id_type=MESH,
        )

    def coords(t):
        return places[t], places[1 - t]

    def device(t, main, side):
        return main * SIDE + side if t == 0 else side * SIDE + main

    def lane_of(t, main, side):
        return pl.ds(pl.multiple_of(device(t, main, side) * LANES, LANES), LANES)

    def blocks_of(main, side):
        return pl.ds((main * SIDE + side) * blocks, blocks)

    def rows_of(h, t):
        return pl.ds(h * half + t * share, share)

    def back(place, copy):
        return (place + SIDE - copy) % SIDE

    for h, part in [(h, part) for h in range(HALVES) for part in range(0, blocks, BATCH)]:
        for first, second, copy in SPREAD:
            for t in range(KINDS):
                main, side = coords(t)
                to_main, to_side = (main + first) % SIDE, (side + second) % SIDE
                remote(
                    coeffs.at[pl.ds(part, BATCH), rows_of(h, t), lane_of(t, back(to_main, copy), to_side)],
                    pieces[h].at[t, copy, pl.ds((main * SIDE + side) * blocks + part, BATCH)],
                    send1.at[h, t], recv1.at[h, t], (device(t, to_main, to_side), my_ta),
                ).start()

    shift_of = blocks.bit_length() - 1
    spread_lanes = lists.shape[1]
    lists[...] = jnp.zeros_like(lists)
    lists[0:2, 0:pair_total] = block_pairs[...]
    lists[2:3, 0:pair_total] = offsets[...]
    lists[MODE:MODE + modes, 0:pair_total] = mode_index[...]
    column_form = jnp.transpose(lists[...])[:pair_total]
    second = column_form[:, 1:2]
    owner = lax.shift_right_logical(second, shift_of)
    serial = lax.broadcasted_iota(jnp.int32, (pair_total, LANES), 0)
    mine = (lax.broadcasted_iota(jnp.int32, (pair_total, LANES), 1) == owner).astype(jnp.int32)
    count = mine
    step = 1
    while step < pair_total:
        count = count + jnp.where(serial >= step, pltpu.roll(count, step, 0), 0)
        step *= 2
    rank = jnp.sum(mine * (count - 1), axis=1, keepdims=True)
    slot = owner * pair_count + rank
    hot = lax.broadcasted_iota(jnp.int32, (pair_total, spread_lanes), 1) == slot
    start = column_form[:, 2:3] + my_ta * trans
    start = jnp.where(start >= trans_all, start - trans_all, start)

    def swap(block):
        owner_of = lax.shift_right_logical(block, shift_of)
        swapped = (owner_of & (SIDE - 1)) * SIDE + lax.shift_right_logical(owner_of, SIDE.bit_length() - 1)
        return swapped * blocks + (block & (blocks - 1))

    columns = [
        column_form[:, 0:1], second, second & (blocks - 1),
        lax.shift_right_logical(start, 7), start & (LANES - 1),
        swap(column_form[:, 0:1]),
    ] + [column_form[:, MODE + m:MODE + m + 1] for m in range(modes)]
    for c, column in enumerate(columns):
        lists[c:c + 1, :] = jnp.sum(jnp.where(hot, column, 0), axis=0, keepdims=True)
    listing = pltpu.make_async_copy(lists.at[pl.ds(0, TILE)], ints, local.at[1])
    listing.start()
    fetch.wait()
    listing.wait()
    for h in range(HALVES):
        for t in range(KINDS):
            main, side = coords(t)
            for copy in range(COPIES):
                pieces[h][t, copy, blocks_of(main, side)] = held[:, rows_of(h, t), lane_of(t, back(main, copy), side)]

    def number(s, which):
        return ints[which, my_pb * pair_count + s]

    def spread_of(h, t):
        part = stage.at[h, t, pl.ds(0, blocks)]
        return remote(part, part, send1.at[h, t], recv1.at[h, t], (far_peers[0], my_ta))

    def copies_of(h, t):
        part = pieces[h].at[t, 0]
        return remote(part, part, send5.at[h, t], recv5.at[h, t], (far_peers[0], my_ta))

    def hand_on(h):
        for t in range(KINDS):
            spread_of(h, t).wait_recv()
        for w in range(SIDE):
            for t in range(KINDS):
                main, side = coords(t)
                for copy, move in ((0, 1), (1, SIDE - 1)):
                    to = (main + move) % SIDE
                    for origin in (main, (main + SIDE - move) % SIDE):
                        remote(
                            pieces[h].at[t, copy, blocks_of(origin, w)], pieces[h].at[t, 1 - copy, blocks_of(origin, w)],
                            send5.at[h, t], recv5.at[h, t], (device(t, to, side), my_ta),
                        ).start()

    def give_out(h):
        for t in range(KINDS):
            copies_of(h, t).wait_recv()

        def piece(t, copy, place, s):
            return pieces[h][t, copy, ints[SWAPPED if t else FIRST, place * pair_count + s]]

        def deliver(s, count):
            for k, (first, second, copy) in enumerate(GIVE):
                for t in range(KINDS):
                    main, side = coords(t)
                    to = device(t, (main + first) % SIDE, (side + second) % SIDE)
                    for u in range(count):
                        stage[h, t, s + u, k] = piece(t, copy, to, s + u)
                    remote(
                        stage.at[h, t, pl.ds(s, count), k],
                        other.at[h, t, pl.ds(s, count), device(t, back(main, copy), side)],
                        send2.at[h, t, s], recv2.at[h, t, s], (to, my_ta),
                    ).start()
            for t in range(KINDS):
                main, side = coords(t)
                for copy in range(COPIES):
                    for u in range(count):
                        other[h, t, s + u, device(t, back(main, copy), side)] = piece(t, copy, my_pb, s + u)

        def deliver_round(g, carry):
            deliver(ROUND * g, ROUND)
            return carry

        def deliver_one(s, carry):
            deliver(s, 1)
            return carry

        singles = SINGLE if h == HALVES - 1 else 0
        lax.fori_loop(0, (pair_count - singles) // ROUND, deliver_round, 0)
        lax.fori_loop(pair_count - singles, pair_count, deliver_one, 0)

    for h in range(HALVES):
        hand_on(h)
    give_out(0)

    wide[...] = jnp.zeros_like(wide)
    tiles_all = trans_all // LANES
    tiles = trans // LANES

    def widen(tile, carry):
        lane = pl.multiple_of(lax.rem(tile, tiles_all) * LANES, LANES)
        wide[tile, pl.ds(0, modes), :] = table[:, pl.ds(lane, LANES)].astype(jnp.float32)
        return carry

    lax.fori_loop(0, wide.shape[0], widen, 0)
    acc_first[...] = jnp.zeros_like(acc_first)
    acc_second[...] = jnp.zeros_like(acc_second)

    def strips_of(source_ref, block):
        row = source_ref[pl.ds(block, 1), :]
        turn[...] = jnp.transpose(jnp.broadcast_to(row, (rows, rows)))
        return [
            turn[pl.ds(pl.multiple_of(h * half + my_ta * strip, strip), strip), :]
            for h in range(HALVES)
        ]

    def prepare(s, carry):
        first, second_one = number(s, FIRST), number(s, SECOND)
        piece = wide[pl.ds(number(s, START), tiles + 1)]
        amount = jnp.full(piece.shape, number(s, SHIFT), jnp.int32)
        for bit in range(7):
            moved = pltpu.roll(piece, LANES - (1 << bit), 2)
            piece = jnp.where((amount & (1 << bit)) != 0, moved, piece)
        keep = lax.broadcasted_iota(jnp.int32, (TILE, LANES), 1) < LANES - amount[0]
        for t in range(tiles):
            window[s, :, t * LANES:(t + 1) * LANES] = jnp.where(keep, piece[t], piece[t + 1])
        energy_b = energies[pl.ds(second_one, 1), :]
        energy_a = strips_of(energies, first)
        for h in range(HALVES):
            detuning = energy_a[h] - energy_b
            for m in range(modes):
                energy = jnp.full(detuning.shape, phonon[m], jnp.float32)
                bose = 1.0 / (jnp.exp(energy / BOLTZMANN_KT) - 1.0)
                minus = 1.0 / (1.0 + ((detuning - energy) / BROADENING) ** 2)
                plus = 1.0 / (1.0 + ((detuning + energy) / BROADENING) ** 2)
                scale = 1.0 / (modes * rows)
                weight_f[s, h, m] = ((bose + 1.0) * minus + bose * plus) * scale
                weight_b[s, h, m] = ((bose + 1.0) * plus + bose * minus) * scale
        for h, value in enumerate(strips_of(deviation, first)):
            value_a[s, h] = value
        return carry

    lax.fori_loop(0, pair_count, prepare, 0)
    for h in range(1, HALVES):
        give_out(h)

    def flows(h, s):
        index = h * pair_count + s
        copy = remote(
            part_in.at[index, pl.ds(0, n_mates)], part_in.at[index, pl.ds(0, n_mates)],
            send3.at[index], recv3.at[index], (my_pb, mates[0]),
        )
        copy.wait_recv()
        coupling = part_in[index, 0].astype(jnp.float32)
        for q in range(1, ta_count):
            coupling = coupling + part_in[index, q].astype(jnp.float32)
        coupling = coupling[:modes * strip].reshape(modes, strip, rows)
        square = coupling * coupling
        forward = jnp.sum(square * weight_f[s, h], axis=0)
        backward = jnp.sum(square * weight_b[s, h], axis=0)
        value_b = deviation[pl.ds(number(s, SECOND), 1), :]
        out_first = jnp.sum(forward, axis=1, keepdims=True)
        in_first = jnp.sum(backward * value_b, axis=1, keepdims=True)
        out_second = jnp.sum(backward, axis=0, keepdims=True)
        in_second = jnp.sum(forward * value_a[s, h], axis=0, keepdims=True)
        here = lax.broadcasted_iota(jnp.int32, (strip, rows), 1) == number(s, FIRST)
        acc_first[0, h] += jnp.where(here, out_first, 0.0)
        acc_first[1, h] += jnp.where(here, in_first, 0.0)
        there = lax.broadcasted_iota(jnp.int32, (blocks, rows), 0) == number(s, PLACE)
        acc_second[0] += jnp.where(there, out_second, 0.0)
        acc_second[1] += jnp.where(there, in_second, 0.0)

    pad = part_out.shape[2] - modes * strip

    def arrival(n, act):
        h, s = n // pair_count, n % pair_count

        def of(t, count):
            part = stage.at[h, t, pl.ds(s, count)]
            return remote(part, part, send2.at[h, t, s], recv2.at[h, t, s], (far_peers[0], my_ta))

        @pl.when((n < paired) & (n % ROUND == 0))
        def _():
            for t in range(KINDS):
                act(of(t, ROUND))

        @pl.when(n >= paired)
        def _():
            for t in range(KINDS):
                act(of(t, 1))

    def couple(n, carry):
        h, s = n // pair_count, n % pair_count

        @pl.when(n >= LAG)
        def _():
            flows((n - LAG) // pair_count, (n - LAG) % pair_count)

        arrival(n, lambda copy: copy.wait_recv())
        index = n
        for m in range(modes):
            row = window[s, pl.ds(number(s, MODE + m), 1), :]
            scale = jnp.broadcast_to(row, (TILE, trans)).astype(jnp.bfloat16)
            for t in range(tiles):
                for kind in range(KINDS):
                    block = other[h, kind, s, t].reshape(share // TILE, TILE, LANES)
                    block = block * scale[None, :, t * LANES:(t + 1) * LANES]
                    low = m * half + kind * share
                    scaled[low:low + share, t * LANES:(t + 1) * LANES] = block.reshape(share, LANES)
        product = lax.dot_general(
            scaled[...], held[number(s, PLACE)],
            (((1,), (1,)), ((), ())), preferred_element_type=jnp.float32,
        ).reshape(modes, ta_count, strip, rows)
        for q in range(ta_count):
            part = jnp.concatenate(
                [product[:, q].reshape(modes * strip, rows), jnp.zeros((pad, rows), jnp.float32)], axis=0
            )
            part_out[index, q] = part.astype(jnp.bfloat16)
        for mate in mates:
            remote(
                part_out.at[index, mate], part_in.at[index, my_ta],
                send3.at[index], recv3.at[index], (my_pb, mate),
            ).start()
        part_in[index, my_ta] = part_out[index, my_ta]
        return carry

    lax.fori_loop(0, HALVES * pair_count, couple, 0)
    for s in range(pair_count - LAG, pair_count):
        flows(HALVES - 1, s)

    used = 2 * HALVES * strip
    stacked = jnp.concatenate(
        [acc_first[...].reshape(used, rows), jnp.zeros((LANES - used, rows), jnp.float32)], axis=0
    )
    first_out[...] = jnp.transpose(stacked)
    for peer in far_peers:
        remote(
            first_out.at[pl.ds(pl.multiple_of(peer * blocks, blocks), blocks)], first_in.at[my_pb],
            send4.at[0], recv4.at[0], (peer, my_ta),
        ).start()
    for mate in mates:
        remote(acc_second, second_in.at[my_ta], send4.at[1], recv4.at[1], (my_pb, mate)).start()
    first_in[my_pb] = first_out[pl.ds(pl.multiple_of(my_pb * blocks, blocks), blocks)]
    second_in[my_ta] = acc_second[...]

    for h in range(HALVES):
        for t in range(KINDS):
            spread_of(h, t).wait_send()
            copies_of(h, t).wait_send()

    def sent(n, carry):
        arrival(n, lambda copy: copy.wait_send())
        block = part_in.at[n, pl.ds(0, n_mates)]
        remote(block, block, send3.at[n], recv3.at[n], (my_pb, mates[0])).wait_send()
        return carry

    lax.fori_loop(0, pair_count, sent, 0)

    few = first_in.at[pl.ds(0, n_peers)]
    sums = remote(few, few, send4.at[0], recv4.at[0], (far_peers[0], my_ta))
    sums.wait_recv()
    total[...] = jnp.sum(first_in[...], axis=0)
    for mate in mates:
        remote(total, total_in.at[my_ta], send4.at[2], recv4.at[2], (my_pb, mate)).start()
    total_in[my_ta] = total[...]
    lax.fori_loop(pair_count, HALVES * pair_count, sent, 0)
    sums.wait_send()
    for ref, sem in ((second_in, 1), (total_in, 2)):
        few = ref.at[pl.ds(0, n_mates)]
        copy = remote(few, few, send4.at[sem], recv4.at[sem], (my_pb, mates[0]))
        copy.wait_send()
        copy.wait_recv()
    lane = lax.broadcasted_iota(jnp.int32, (blocks, LANES), 1)
    for c in range(2):
        flow = jnp.sum(second_in[:, c], axis=0)
        for h in range(HALVES):
            low = (c * HALVES + h) * strip
            inside = (lane >= low) & (lane < low + strip)
            for q in range(ta_count):
                target = h * half + q * strip
                part = jnp.where(inside, total_in[q], 0.0)
                flow = flow + pltpu.roll(part, (target - low) % LANES, 1)
        flow_out[c] = flow


def shards(
    coeffs,
    elph_table,
    energies,
    phonon_energy,
    deviation,
    source,
    inv_tau,
    block_pairs,
    mode_index,
    offsets,
):
    blocks, rows, trans = coeffs.shape
    modes, trans_all = elph_table.shape
    pair_total = block_pairs.shape[0]
    pb_count = lax.axis_size("pb")
    ta_count = lax.axis_size("ta")
    half = rows // HALVES
    share = half // KINDS
    strip = half // ta_count
    units = HALVES * PAIRS_DEV
    padded = -(-modes * strip // TILE) * TILE
    list_lanes = -(-pair_total // LANES) * LANES
    smem = pl.BlockSpec(memory_space=pltpu.SMEM)
    vmem = pl.BlockSpec(memory_space=pltpu.VMEM)
    f32, bf16 = jnp.float32, jnp.bfloat16
    dma = pltpu.SemaphoreType.DMA
    flow = pl.pallas_call(
        kernel,
        out_shape=pltpu.VMEM((2, blocks, rows), f32),
        in_specs=[smem, pl.BlockSpec(memory_space=pl.ANY)] + [vmem] * 6,
        out_specs=vmem,
        scratch_shapes=[
            pltpu.VMEM((blocks, rows, trans), bf16),
            pltpu.VMEM((KINDS, COPIES, pb_count * blocks, share, LANES), bf16),
            pltpu.VMEM((KINDS, COPIES, pb_count * blocks, share, LANES), bf16),
            pltpu.VMEM((HALVES, KINDS, PAIRS_DEV, len(GIVE), share, LANES), bf16),
            pltpu.VMEM((HALVES, KINDS, PAIRS_DEV, pb_count, share, LANES), bf16),
            pltpu.VMEM((modes * half, trans), bf16),
            pltpu.VMEM((units, ta_count, padded, rows), bf16),
            pltpu.VMEM((units, ta_count, padded, rows), bf16),
            pltpu.VMEM((PAIRS_DEV, HALVES, modes, strip, rows), f32),
            pltpu.VMEM((PAIRS_DEV, HALVES, modes, strip, rows), f32),
            pltpu.VMEM((PAIRS_DEV, HALVES, strip, rows), f32),
            pltpu.VMEM(((trans_all + trans) // LANES + 1, TILE, LANES), f32),
            pltpu.VMEM((PAIRS_DEV, TILE, trans), f32),
            pltpu.VMEM((rows, rows), f32),
            pltpu.VMEM((LANES, list_lanes), jnp.int32),
            pltpu.SMEM((TILE, list_lanes), jnp.int32),
            pltpu.VMEM((2, HALVES, strip, rows), f32),
            pltpu.VMEM((2, blocks, rows), f32),
            pltpu.VMEM((pb_count * blocks, LANES), f32),
            pltpu.VMEM((pb_count, blocks, LANES), f32),
            pltpu.VMEM((ta_count, 2, blocks, rows), f32),
            pltpu.VMEM((blocks, LANES), f32),
            pltpu.VMEM((ta_count, blocks, LANES), f32),
            dma((2,)),
            dma((HALVES, KINDS)), dma((HALVES, KINDS)),
            dma((HALVES, KINDS, PAIRS_DEV)), dma((HALVES, KINDS, PAIRS_DEV)),
            dma((units,)), dma((units,)),
            dma((3,)), dma((3,)),
            dma((HALVES, KINDS)), dma((HALVES, KINDS)),
        ],
        compiler_params=pltpu.CompilerParams(
            collective_id=0, has_side_effects=True, vmem_limit_bytes=56 << 20
        ),
        name="rates",
    )(
        phonon_energy, coeffs, elph_table, energies, deviation, block_pairs.T, mode_index.T,
        offsets.reshape(1, pair_total),
    )
    return (source + flow[1]) / (inv_tau + flow[0]), flow[0]


def solution(mesh):
    in_specs = (
        P("pb", None, "ta"),
        P(),
        P(),
        P(),
        P(),
        P("pb", None),
        P("pb", None),
        P(),
        P(),
        P(),
    )
    out_specs = (P("pb", None), P("pb", None))
    return jax.shard_map(shards, mesh=mesh, in_specs=in_specs, out_specs=out_specs, check_vma=False)
```
